128 devices in a mesh: dp: 16 (over z, x_lo, core), head: 8 (over y, x_hi).
Axes of the slice: x: 4 (x_hi: 2, x_lo: 2; x = x_hi * 2 + x_lo), y: 4, z: 4, core: 2. Of those that a mesh axis runs over, the one named last changes fastest.
Arguments:
- query: bfloat16 [16384, 4096], P(('dp', 'head')), may hold values from -6 to 6
- key_states: bfloat16 [16384, 1024], P(('dp', 'head')), may hold values from -6 to 6
- value_states: bfloat16 [16384, 1024], P(('dp', 'head')), may hold values from -6 to 6
- grad_attended: bfloat16 [16384, 4096], P(('dp', 'head')), may hold values from -6 to 6
- query_gain: float32 [128], replicated, may hold values from 0.6 to 5.5
- key_gain: float32 [128], replicated, may hold values from 0.6 to 5.5
- doc_lengths: int32 [16, 8], replicated, may hold values from 1 to 512, 1024 in all within a row
Outputs:
- attended: bfloat16 [16384, 4096], P(('dp', 'head'))
- grad_query: bfloat16 [16384, 4096], P(('dp', 'head'))
- grad_key: bfloat16 [16384, 1024], P(('dp', 'head'))
- grad_value: bfloat16 [16384, 1024], P(('dp', 'head'))
- grad_query_gain: float32 [128], replicated
- grad_key_gain: float32 [128], replicated
The draws below stay inside these ranges and needn't reach their ends.
Inputs may be any that keep to these rules, and one draw needn't show every extreme that they name: `doc_lengths`: each row sums to 1024.
All inputs are finite; a program needn't handle non-finite values.
Results may differ from the reference program's by a relative error of at most 0.007.
The reference program's roundings to bfloat16 on the way (of `dscores`) count: a program that leaves them out, or rounds other values in their place, can miss the bound.
Values may be sent and summed in bfloat16 or wider, within the bound.
No kernel may reach another device: no remote copies, remote signals or barrier semaphores. Data moves between devices by JAX's collectives and lax.ppermute only.
A program may use at most 192 MiB of HBM per device.

```python
import math
import jax
import jax.numpy as jnp
import numpy as np
from jax import lax

H = 32
KVH = 8
HD = 128
DOCS = 8
TOK_REP = 1024
TOKENS = 16384
MOST_DOC = 512
N_DP = 16


def shared_keys(key):
    return jax.random.normal(key, (TOKENS, KVH * HD), jnp.float32)


def draw_key_states(key, part):
    base = shared_keys(key)
    return jnp.clip(base, -6.0, 6.0).astype(jnp.bfloat16)


def draw_query(key, part):
    key = jax.random.fold_in(key, 7)
    fresh = jax.random.normal(key, (TOKENS, H * HD), jnp.float32)
    return jnp.clip(fresh, -6.0, 6.0).astype(jnp.bfloat16)


def gain_values(key, lower, upper):
    return jax.random.uniform(key, (HD,), jnp.float32, lower, upper)


def draw_query_gain(key, part):
    key = jax.random.fold_in(key, 3)
    return gain_values(key, 0.6, 1.6)


def draw_key_gain(key, part):
    key = jax.random.fold_in(key, 5)
    return gain_values(key, 0.6, 1.6)


def level_of(stream_key, dims, cuts, low, high):
    def one(position, blocks):
        heights = jax.random.uniform(jax.random.fold_in(jax.random.fold_in(stream_key, 6), position), (blocks,), jnp.float32, low / len(cuts), high / len(cuts))
        return jnp.repeat(jnp.exp(heights), dims[position] // blocks).reshape((-1,) + (1,) * (len(dims) - position - 1))

    level = one(*cuts[0])
    for cut in cuts[1:]:
        level = level * one(*cut)
    return level


def length_profile(amount, total, most, skew):
    weights = [(1 << 20) // math.isqrt(rank ** skew) + 1 for rank in range(2, amount + 1)]
    rest, holding = total - most - (amount - 1), [1] * (amount - 1)
    while rest > 0:
        movable = [i for i in range(amount - 1) if holding[i] < most]
        mass, remaining = sum([weights[i] for i in movable]), rest
        for i in movable:
            more = min(most - holding[i], max(1, remaining * weights[i] // mass), rest)
            holding[i] = holding[i] + more
            rest = rest - more
    return np.array([most] + holding)


def ragged(stream_key, amount, total, reach, skew):
    if amount == 2:
        one = jax.random.randint(stream_key, (), max(1, total - reach), min(reach, total - 1) + 1)
        return jnp.stack([one, total - one])
    tallies = jnp.asarray(length_profile(amount, total, reach, skew), jnp.int32)
    pairs = (amount - 1) // 2
    source_of, receiver = tallies[1:1 + 2 * pairs:2], tallies[2:2 + 2 * pairs:2]
    margin = jnp.minimum(source_of - 1, reach - receiver)
    moved = jax.random.randint(jax.random.fold_in(stream_key, 1), (pairs,), 0, 1 << 20) % (margin + 1)
    tallies = tallies.at[1:1 + 2 * pairs:2].set(source_of - moved).at[2:2 + 2 * pairs:2].set(receiver + moved)
    return tallies[jax.random.permutation(jax.random.fold_in(stream_key, 2), amount)]


def centred(own_key, extent, width, reach, shards=(), kind=jnp.bfloat16):
    values = width * jax.random.normal(own_key, extent, jnp.float32)
    if shards:
        values = values * level_of(own_key, extent, shards, -0.22, 0.18)
    return jnp.clip(values, -reach, reach).astype(kind)


def setup_inputs(seed: int = 0) -> dict:
    splits = jax.random.split(jax.random.key(seed), 8)
    query = draw_query(jax.random.fold_in(splits[7], 71), 0)
    key_states = draw_key_states(jax.random.fold_in(splits[7], 71), 0)
    value_states = centred(splits[2], (TOKENS, KVH * HD), 1.0, 6.0, ((0, 128),))
    grad_attended = centred(splits[3], (TOKENS, H * HD), 1.0, 6.0, ((0, 128),))
    query_gain = draw_query_gain(jax.random.fold_in(splits[7], 71), 0)
    key_gain = draw_key_gain(jax.random.fold_in(splits[7], 71), 0)
    doc_lengths = jax.vmap(lambda own: ragged(own, DOCS, TOK_REP, MOST_DOC, 2))(jax.random.split(splits[6], N_DP)).reshape((N_DP, DOCS)).astype(jnp.int32)
    return {"query": query, "key_states": key_states, "value_states": value_states, "grad_attended": grad_attended, "query_gain": query_gain, "key_gain": key_gain, "doc_lengths": doc_lengths}


def product(form, left, right):
    return jnp.einsum(form, left.astype(jnp.float32), right.astype(jnp.float32))

def normalize(raw, gain):
    values = raw.astype(jnp.float32)
    inverse = lax.rsqrt(lax.optimization_barrier(jnp.mean(values * values, axis=-1, keepdims=True)) + 1e-06)
    unit_vals = values * inverse
    return ((unit_vals * gain).astype(jnp.bfloat16), unit_vals, inverse)

def norm_grad(grad_normed, unit_vals, inverse, gain):
    scaled = grad_normed * gain
    back = inverse * (scaled - unit_vals * lax.optimization_barrier(jnp.mean(scaled * unit_vals, axis=-1, keepdims=True)))
    partial_sum = lax.optimization_barrier(jnp.sum(grad_normed * unit_vals, axis=tuple(range(unit_vals.ndim - 1))))
    return (back.astype(jnp.bfloat16), partial_sum)

def attend(normed_q, normed_k, values, grads, q_labels, q_places, k_labels, k_places):
    q_len, groups, per_group, head_dim = normed_q.shape
    factor = head_dim ** (-0.5)
    step_rows = min(512, q_len)
    out_blocks = []
    dq_blocks = []
    dk_parts = [jnp.zeros((normed_k.shape[0], head_dim), jnp.float32) for member in range(groups)]
    dv_parts = [jnp.zeros((normed_k.shape[0], head_dim), jnp.float32) for member in range(groups)]
    for start in range(0, q_len, step_rows):
        stop = start + step_rows
        allowed = (q_labels[start:stop, None] == k_labels[None, :]) & (k_places[None, :] <= q_places[start:stop, None])
        out_heads = []
        dq_heads = []
        for member in range(groups):
            q_here = normed_q[start:stop, member]
            k_here = normed_k[:, member]
            v_here = values[:, member]
            g_here = grads[start:stop, member]
            scores = product('bgd,kd->gbk', q_here, k_here) * factor
            scores = jnp.where(allowed[None], scores, -1e+30)
            peak = lax.optimization_barrier(jnp.max(scores, axis=2, keepdims=True))
            raised = jnp.exp(scores - peak)
            weights = raised / lax.optimization_barrier(jnp.sum(raised, axis=2, keepdims=True))
            rounded = weights.astype(jnp.bfloat16)
            result = product('gbk,kd->bgd', rounded, v_here)
            dv_parts[member] = dv_parts[member] + product('gbk,bgd->kd', rounded, g_here)
            dweights = product('bgd,kd->gbk', g_here, v_here)
            delta = lax.optimization_barrier(jnp.sum(g_here.astype(jnp.float32) * result, axis=2))
            dscores = (weights * (dweights - jnp.transpose(delta)[:, :, None]) * factor).astype(jnp.bfloat16)
            dq_heads.append(product('gbk,kd->bgd', dscores, k_here))
            dk_parts[member] = dk_parts[member] + product('gbk,bgd->kd', dscores, q_here)
            out_heads.append(result)
        out_blocks.append(jnp.stack(out_heads, axis=1))
        dq_blocks.append(jnp.stack(dq_heads, axis=1))
    return (jnp.concatenate(out_blocks, axis=0), jnp.concatenate(dq_blocks, axis=0), jnp.stack(dk_parts, axis=1), jnp.stack(dv_parts, axis=1))

def reference(query, key_states, value_states, grad_attended, query_gain, key_gain, doc_lengths):
    group = H // KVH
    moved = [item.reshape(N_DP, TOK_REP, item.shape[-1]) for item in (query, key_states, value_states, grad_attended)]
    ends = jnp.cumsum(doc_lengths, axis=1)
    places = jnp.arange(TOK_REP, dtype=jnp.int32)
    before = lax.optimization_barrier(jnp.sum((ends[:, None, :] <= places[None, :, None]).astype(jnp.int32), axis=2))
    labels = before + (jnp.arange(N_DP, dtype=jnp.int32) * doc_lengths.shape[1])[:, None]

    def one_replica(items):
        q_rows, k_rows, v_rows, g_rows, label_row = items
        normed_q, q_unit, q_inverse = normalize(q_rows.reshape(TOK_REP, KVH, group, HD), query_gain)
        normed_k, k_unit, k_inverse = normalize(k_rows.reshape(TOK_REP, KVH, HD), key_gain)
        outs, dq_normed, dk_normed, dv_sum = attend(normed_q, normed_k, v_rows.reshape(TOK_REP, KVH, HD), g_rows.reshape(TOK_REP, KVH, group, HD), label_row, places, label_row, places)
        dq_rows, q_part = norm_grad(dq_normed, q_unit, q_inverse, query_gain)
        dk_rows, k_part = norm_grad(dk_normed, k_unit, k_inverse, key_gain)
        return (outs.astype(jnp.bfloat16).reshape(TOK_REP, H * HD), dq_rows.reshape(TOK_REP, H * HD), dk_rows.reshape(TOK_REP, KVH * HD), dv_sum.astype(jnp.bfloat16).reshape(TOK_REP, KVH * HD), q_part, k_part)
    results = lax.map(one_replica, (moved[0], moved[1], moved[2], moved[3], labels))
    finals = [item.reshape(TOKENS, item.shape[-1]) for item in results[:4]]
    q_total = lax.optimization_barrier(jnp.sum(results[4], axis=0)) * (TOKENS * H) ** (-0.5)
    k_total = lax.optimization_barrier(jnp.sum(results[5], axis=0)) * (TOKENS * KVH) ** (-0.5)
    return (finals[0], finals[1], finals[2], finals[3], q_total, k_total)
```

```python
import functools
import math

import jax
import jax.numpy as jnp
from jax import lax
from jax.experimental import pallas as pl
from jax.experimental.pallas import tpu as pltpu
from jax.sharding import PartitionSpec as P

H = 32
KVH = 8
HD = 128
GROUP = H // KVH
MOST_DOC = 512
BLK = 128
WINDOWS = MOST_DOC // BLK + 1
EPS = 1e-06
FACTOR = HD ** (-0.5)
EXP2_FACTOR = FACTOR * math.log2(math.e)
CHUNKS = ((0, 4),)
F32 = jnp.float32
BF16 = jnp.bfloat16


def dot(left, right, contract):
    return lax.dot_general(left, right, ((contract[:1], contract[1:]), ((), ())), preferred_element_type=F32)


def copies_kernel(plan, n_in, *refs):
    sems = refs[-1]
    moves = []
    for i, (src, src_at, dst, dst_at) in enumerate(plan):
        moves.append(pltpu.make_async_copy(refs[src].at[src_at], refs[n_in + dst].at[dst_at], sems.at[i]))
    for move in moves:
        move.start()
    for move in moves:
        move.wait()


def run_copies(plan, arrays, shapes, sources, targets):
    return pl.pallas_call(
        functools.partial(copies_kernel, plan, len(arrays)),
        out_shape=[jax.ShapeDtypeStruct(s, BF16) for s in shapes],
        in_specs=[pl.BlockSpec(memory_space=sources)] * len(arrays),
        out_specs=[pl.BlockSpec(memory_space=targets)] * len(shapes),
        scratch_shapes=[pltpu.SemaphoreType.DMA((len(plan),))],
        compiler_params=pltpu.CompilerParams(vmem_limit_bytes=32 * 1024 * 1024),
    )(*arrays)


def cols(first, width):
    return pl.ds(first, width)


def pack(query, key_states, value_states, grad_attended, chunk, first, members):
    rows = query.shape[0]
    start, count = chunk
    width = count * HD
    plan = []
    allrows = pl.ds(0, rows)
    base = 2 * HD if first else 0
    for m in range(members):
        if first:
            plan.append((0, (allrows, cols(m * HD, HD)), 0, (m, allrows, cols(0, HD))))
            plan.append((1, (allrows, cols(m * HD, HD)), 0, (m, allrows, cols(HD, HD))))
        at = (m * GROUP + start) * HD
        plan.append((2, (allrows, cols(at, width)), 0, (m, allrows, cols(base, width))))
        plan.append((3, (allrows, cols(at, width)), 0, (m, allrows, cols(base + width, width))))
    shape = (members, rows, base + 2 * width)
    return run_copies(
        plan, (key_states, value_states, query, grad_attended), [shape], pl.ANY, pltpu.VMEM
    )[0]


def unpack(parts, members, rows):
    plan = []
    allrows = pl.ds(0, rows)
    for index, (start, count) in enumerate(CHUNKS):
        width = count * HD
        for m in range(members):
            at = (m * GROUP + start) * HD
            plan.append((index, (m, allrows, cols(0, width)), 0, (allrows, cols(at, width))))
            plan.append((index, (m, allrows, cols(width, width)), 1, (allrows, cols(at, width))))
            if index == len(CHUNKS) - 1:
                plan.append((index, (m, allrows, cols(2 * width, HD)), 2, (allrows, cols(m * HD, HD))))
                plan.append((index, (m, allrows, cols(2 * width + HD, HD)), 3, (allrows, cols(m * HD, HD))))
    shapes = [(rows, H * HD), (rows, H * HD), (rows, KVH * HD), (rows, KVH * HD)]
    return run_copies(plan, parts, shapes, pltpu.VMEM, pl.ANY)


def unit_of(raw):
    values = raw.astype(F32)
    inverse = lax.rsqrt(jnp.mean(values * values, axis=-1, keepdims=True) + EPS)
    return values * inverse, inverse


def attend_kernel(count, first, last, *refs):
    refs = list(refs)
    lengths_ref, q_gain_ref, k_gain_ref, kv_ref = refs[:4]
    del refs[:4]
    x_ref = kv_ref if first else refs.pop(0)
    if not first:
        dk_in, dv_in, gains_in = refs[:3]
        del refs[:3]
    y_ref = refs.pop(0)
    if not last:
        dk_ref, dv_ref = refs[:2]
        del refs[:2]
    gains_ref = refs.pop(0)
    if last:
        dk_ref, dv_ref = refs[:2]
        del refs[:2]
    kn_ref, qn_ref, g_ref, out_ref, dq_ref, bias_ref = refs
    base = 2 * HD if first else 0
    width = count * HD
    span = kv_ref.shape[0]
    replica = lax.axis_index("dp")
    q_gain = q_gain_ref[...]
    k_gain = k_gain_ref[...]

    k_unit, _ = unit_of(kv_ref[:, :HD])
    kn_ref[...] = (k_unit * k_gain).astype(BF16)
    if first:
        dk_ref[...] = jnp.zeros_like(dk_ref)
        dv_ref[...] = jnp.zeros_like(dv_ref)
        gains_ref[...] = jnp.zeros_like(gains_ref)
    else:
        dk_ref[...] = dk_in[...]
        dv_ref[...] = dv_in[...]
        gains_ref[...] = gains_in[...]
    ends = []
    total = jnp.int32(0)
    for d in range(lengths_ref.shape[1]):
        total = total + lengths_ref[replica, d]
        ends.append(total)

    def block(i, carry):
        row0 = pl.multiple_of(i * BLK, BLK)
        rows = pl.ds(row0, BLK)
        places = row0 + lax.broadcasted_iota(jnp.int32, (BLK, BLK), 0)
        begins = jnp.zeros((BLK, BLK), jnp.int32)
        begin0 = jnp.int32(0)
        for end in ends:
            begins = jnp.where(end <= places, end, begins)
            begin0 = jnp.where(end <= row0, end, begin0)
        first_block = begin0 // BLK
        needed = i - first_block + 1
        units = []
        for h in range(count):
            unit, inverse = unit_of(x_ref[rows, base + h * HD : base + (h + 1) * HD])
            units.append((unit, inverse))
            qn_ref[h * BLK : (h + 1) * BLK, :] = (unit * q_gain).astype(BF16)
            g_ref[h * BLK : (h + 1) * BLK, :] = x_ref[
                rows, base + width + h * HD : base + width + (h + 1) * HD
            ]
        for blocks in range(1, WINDOWS + 1):

            @pl.when(needed == blocks)
            def _():
                keys = blocks * BLK
                k0 = pl.multiple_of(first_block * BLK, BLK)
                window = pl.ds(k0, keys)
                lane = k0 + lax.broadcasted_iota(jnp.int32, (BLK, BLK), 1)
                for t in range(blocks):
                    place = lane + t * BLK
                    seen = place >= begins
                    if t == blocks - 1:
                        seen = seen & (place <= places)
                    bias_ref[:, t * BLK : (t + 1) * BLK] = jnp.where(seen, 0.0, -1e30)
                qn = qn_ref[...]
                g = g_ref[...]
                kn = kn_ref[window, :]
                v = kv_ref[window, HD : 2 * HD]
                bias = bias_ref[:, :keys]
                scores = dot(qn, kn, (1, 1)).reshape(count, BLK, keys) + bias[None]
                scores = scores.reshape(count * BLK, keys)
                peak = jnp.max(scores, axis=1, keepdims=True)
                raised = jnp.exp2((scores - peak) * EXP2_FACTOR)
                weights = raised * (1.0 / jnp.sum(raised, axis=1, keepdims=True))
                rounded = weights.astype(BF16)
                out = dot(rounded, v, (1, 0))
                out_ref[...] = out
                dv_ref[window, :] += dot(rounded, g, (0, 0))
                dweights = dot(g, v, (1, 1))
                delta = jnp.sum(g.astype(F32) * out, axis=1, keepdims=True)
                dscores = (weights * (dweights - delta) * FACTOR).astype(BF16)
                dq_ref[...] = dot(dscores, kn, (1, 0))
                dk_ref[window, :] += dot(dscores, qn, (0, 0))

        part = jnp.zeros((8, HD), F32)
        for h in range(count):
            unit, inverse = units[h]
            here = slice(h * BLK, (h + 1) * BLK)
            y_ref[rows, h * HD : (h + 1) * HD] = out_ref[here, :].astype(BF16)
            dq = dq_ref[here, :]
            scaled = dq * q_gain
            back = inverse * (scaled - unit * jnp.mean(scaled * unit, axis=-1, keepdims=True))
            y_ref[rows, width + h * HD : width + (h + 1) * HD] = back.astype(BF16)
            part = part + jnp.sum((dq * unit).reshape(BLK // 8, 8, HD), axis=0)
        gains_ref[0:8, :] += part
        return carry

    lax.fori_loop(0, span // BLK, block, 0)

    if last:
        for r in range(0, span, BLK):
            rows = slice(r, r + BLK)
            unit, inverse = unit_of(kv_ref[rows, :HD])
            dk = dk_ref[rows, :]
            scaled = dk * k_gain
            back = inverse * (scaled - unit * jnp.mean(scaled * unit, axis=-1, keepdims=True))
            y_ref[rows, 2 * width : 2 * width + HD] = back.astype(BF16)
            y_ref[rows, 2 * width + HD : 2 * width + 2 * HD] = dv_ref[rows, :].astype(BF16)
            gains_ref[8:16, :] += jnp.sum((dk * unit).reshape(BLK // 8, 8, HD), axis=0)


def run_attend(lengths, q_gain, k_gain, kv, x, before, count, last):
    first = x is None
    span = kv.shape[0]
    vmem = pl.BlockSpec(memory_space=pltpu.VMEM)
    args = [lengths, q_gain, k_gain, kv]
    if not first:
        args += [x, *before]
    sums = jax.ShapeDtypeStruct((span, HD), F32)
    out_shape = [jax.ShapeDtypeStruct((span, 2 * count * HD + (2 * HD if last else 0)), BF16)]
    if not last:
        out_shape += [sums, sums]
    out_shape += [jax.ShapeDtypeStruct((16, HD), F32)]
    scratch = [pltpu.VMEM((span, HD), F32)] * 2 if last else []
    scratch += [
        pltpu.VMEM((span, HD), BF16),
        pltpu.VMEM((count * BLK, HD), BF16),
        pltpu.VMEM((count * BLK, HD), BF16),
        pltpu.VMEM((count * BLK, HD), F32),
        pltpu.VMEM((count * BLK, HD), F32),
        pltpu.VMEM((BLK, WINDOWS * BLK), F32),
    ]
    return pl.pallas_call(
        functools.partial(attend_kernel, count, first, last),
        out_shape=out_shape,
        in_specs=[pl.BlockSpec(memory_space=pltpu.SMEM)] + [vmem] * (len(args) - 1),
        out_specs=[vmem] * len(out_shape),
        scratch_shapes=scratch,
        compiler_params=pltpu.CompilerParams(vmem_limit_bytes=48 * 1024 * 1024),
        cost_estimate=pl.CostEstimate(
            flops=5 * 2 * count * span * 384 * HD, bytes_accessed=4 * span * count * HD * 2, transcendentals=count * span * 384
        ),
    )(*args)


def sum_everywhere(x):
    for axis, bits in (("dp", (0, 2, 3, 1)), ("head", (0, 1, 2))):
        size = lax.axis_size(axis)
        for bit in bits:
            x = x + lax.ppermute(x, axis, [(i, i ^ 1 << bit) for i in range(size)])
    return x


def on_device(query, key_states, value_states, grad_attended, query_gain, key_gain, doc_lengths):
    replicas = lax.axis_size("dp")
    members = lax.axis_size("head")
    rows = query.shape[0]
    span = rows * members
    q_gain = query_gain.reshape(1, HD)
    k_gain = key_gain.reshape(1, HD)
    arrived = []
    for index, chunk in enumerate(CHUNKS):
        packed = pack(query, key_states, value_states, grad_attended, chunk, index == 0, members)
        moved = lax.all_to_all(packed, "head", split_axis=0, concat_axis=0, tiled=True)
        arrived.append(moved.reshape(span, packed.shape[2]))
    before = None
    results = []
    for index, (_, count) in enumerate(CHUNKS):
        last = index == len(CHUNKS) - 1
        x = None if index == 0 else arrived[index]
        y, *before = run_attend(doc_lengths, q_gain, k_gain, arrived[0], x, before, count, last)
        results.append(
            lax.all_to_all(
                y.reshape(members, rows, y.shape[1]), "head", split_axis=0, concat_axis=0, tiled=True
            )
        )
    gains = before[-1]
    totals = sum_everywhere(
        jnp.stack([jnp.sum(gains[:8], axis=0), jnp.sum(gains[8:], axis=0)])
    )
    finals = unpack(results, members, rows)
    all_tokens = rows * replicas * members
    return (
        *finals,
        totals[0] * (all_tokens * H) ** (-0.5),
        totals[1] * (all_tokens * KVH) ** (-0.5),
    )


def solution(mesh):
    rows = P(("dp", "head"), None)
    in_specs = (rows, rows, rows, rows, P(), P(), P())
    out_specs = (rows, rows, rows, rows, P(), P())
    return jax.shard_map(
        on_device, mesh=mesh, in_specs=in_specs, out_specs=out_specs, check_vma=False
    )
```

```python
import functools
import math

import jax
import jax.numpy as jnp
from jax import lax
from jax.experimental import pallas as pl
from jax.experimental.pallas import tpu as pltpu
from jax.sharding import PartitionSpec as P

H = 32
KVH = 8
HD = 128
GROUP = H // KVH
MOST_DOC = 512
BLK = 128
WINDOWS = MOST_DOC // BLK + 1
YS = 4
PARTS = KVH // YS
WIDTH = GROUP * HD
TAIL = 16
EPS = 1e-06
FACTOR = HD ** (-0.5)
EXP2_FACTOR = FACTOR * math.log2(math.e)
F32 = jnp.float32
BF16 = jnp.bfloat16
HBM = pltpu.HBM
VMEM = pltpu.VMEM
PACK_LIMIT = pltpu.CompilerParams(vmem_limit_bytes=60 * 1024 * 1024)
LIMIT = pltpu.CompilerParams(vmem_limit_bytes=20 * 1024 * 1024)


def dot(left, right, contract):
    return lax.dot_general(left, right, ((contract[:1], contract[1:]), ((), ())), preferred_element_type=F32)


def specs(spaces):
    return [pl.BlockSpec(memory_space=space) for space in spaces]


def shape(rows, columns, kind=BF16):
    return jax.ShapeDtypeStruct((rows, columns), kind)


def my_y():
    return lax.axis_index("head") // 2


def ahead(step):
    return lax.rem(my_y() + step, YS)


def behind(step):
    return lax.rem(my_y() + (YS - step), YS)


def block_rows(index):
    return pl.ds(pl.multiple_of(index * BLK, BLK), BLK)


def do_copies(moves, sems):
    started = [pltpu.make_async_copy(a, b, sems.at[i]) for i, (a, b) in enumerate(moves)]
    for move in started:
        move.start()
    for move in started:
        move.wait()


def pack_kv_kernel(k_ref, v_ref, *refs):
    kv, sems = refs[:YS], refs[YS]
    wide = PARTS * HD
    moves = []
    for step in range(YS):
        at = pl.ds(pl.multiple_of(ahead(step) * wide, wide), wide)
        moves.append((k_ref.at[:, at], kv[step].at[:, pl.ds(0, wide)]))
        moves.append((v_ref.at[:, at], kv[step].at[:, pl.ds(wide, wide)]))
    do_copies(moves, sems)


def pack_qg_kernel(q_ref, g_ref, _, *refs):
    soon, qg, sems = refs[0], refs[1 : 1 + YS], refs[1 + YS]
    moves = []
    for y in range(YS):
        at = pl.ds(y * (PARTS * WIDTH), WIDTH)
        moves.append((q_ref.at[:, at], soon.at[y, :, pl.ds(0, WIDTH)]))
        moves.append((g_ref.at[:, at], soon.at[y, :, pl.ds(WIDTH, WIDTH)]))
    for step in range(YS):
        at = pl.ds(pl.multiple_of(ahead(step) * (PARTS * WIDTH) + WIDTH, WIDTH), WIDTH)
        moves.append((q_ref.at[:, at], qg[step].at[:, pl.ds(0, WIDTH)]))
        moves.append((g_ref.at[:, at], qg[step].at[:, pl.ds(WIDTH, WIDTH)]))
    do_copies(moves, sems)


def after_kernel(*refs):
    pass


def after(x, first):
    return pl.pallas_call(
        after_kernel,
        out_shape=jax.ShapeDtypeStruct(x.shape, x.dtype),
        in_specs=specs([pl.ANY] * 2),
        out_specs=specs([pl.ANY])[0],
        input_output_aliases={0: 0},
    )(x, first)


def gather_kv_kernel(q_gain_ref, k_gain_ref, *refs):
    out, gains_ref = refs[YS:]
    gains_ref[0:1, :] = q_gain_ref[...]
    gains_ref[1:2, :] = k_gain_ref[...]
    for step in range(YS):
        out[block_rows(behind(step)), :] = refs[step][...]


def unit_of(raw):
    values = raw.astype(F32)
    inverse = lax.rsqrt(jnp.mean(values * values, axis=-1, keepdims=True) + EPS)
    return values * inverse, inverse


def norm_back(grad, unit, inverse, gain):
    scaled = grad * gain
    return inverse * (scaled - unit * jnp.mean(scaled * unit, axis=-1, keepdims=True))


def fold(x):
    return jnp.sum(x.reshape(x.shape[0] // 8, 8, x.shape[1]), axis=0)


def attend_kernel(part, *refs):
    refs = list(refs)
    lengths_ref, both_gains_ref, own_ref, far_ref = refs[:4]
    del refs[:4]
    if part == 0:
        qg_ref, y_ref, far_out, own_out, gains_ref = refs[:5]
        del refs[:5]
    else:
        pieces = refs[:YS]
        y_before, far_before, own_before, gains_before = refs[YS : YS + 4]
        del refs[: YS + 4]
        outs = refs[:YS]
        far_out, own_out, gains_ref = refs[YS : YS + 3]
        del refs[: YS + 3]
        qg_ref = refs.pop()
        y_ref = refs.pop()
    kn_ref, v_ref, dk_ref, dv_ref, qn_ref, g_ref, out_ref, dq_ref, bias_ref = refs
    replica = lax.axis_index("dp")
    column = lax.rem(lax.axis_index("head"), 2)
    q_gain = both_gains_ref[0:1, :]
    k_gain = both_gains_ref[1:2, :]
    k_at = slice(part * HD, (part + 1) * HD)
    v_at = slice((PARTS + part) * HD, (PARTS + part + 1) * HD)
    for j in range(YS):
        local = slice(j * BLK, (j + 1) * BLK)
        for ref, col in ((own_ref, column), (far_ref, 1 - column)):
            place = block_rows(2 * j + col)
            unit, _ = unit_of(ref[local, k_at])
            kn_ref[place, :] = (unit * k_gain).astype(BF16)
            v_ref[place, :] = ref[local, v_at]
    if part > 0:
        for step in range(YS):
            qg_ref[block_rows(behind(step)), :] = pieces[step][...]
    dk_ref[...] = jnp.zeros_like(dk_ref)
    dv_ref[...] = jnp.zeros_like(dv_ref)
    ends = []
    total = jnp.int32(0)
    for d in range(lengths_ref.shape[1]):
        total = total + lengths_ref[replica, d]
        ends.append(total)

    def block(j, q_sum):
        here = block_rows(j)
        i = 2 * j + column
        row0 = i * BLK
        places = row0 + lax.broadcasted_iota(jnp.int32, (BLK, BLK), 0)
        begins = jnp.zeros((BLK, BLK), jnp.int32)
        begin0 = jnp.int32(0)
        for end in ends:
            begins = jnp.where(end <= places, end, begins)
            begin0 = jnp.where(end <= row0, end, begin0)
        first_block = begin0 // BLK
        needed = i - first_block + 1
        units = []
        for h in range(GROUP):
            unit, inverse = unit_of(qg_ref[here, h * HD : (h + 1) * HD])
            units.append((unit, inverse))
            qn_ref[h * BLK : (h + 1) * BLK, :] = (unit * q_gain).astype(BF16)
            g_ref[h * BLK : (h + 1) * BLK, :] = qg_ref[here, WIDTH + h * HD : WIDTH + (h + 1) * HD]
        for blocks in range(1, WINDOWS + 1):

            @pl.when(needed == blocks)
            def _():
                keys = blocks * BLK
                k0 = pl.multiple_of(first_block * BLK, BLK)
                window = pl.ds(k0, keys)
                lane = k0 + lax.broadcasted_iota(jnp.int32, (BLK, BLK), 1)
                for t in range(blocks):
                    place = lane + t * BLK
                    seen = place >= begins
                    if t == blocks - 1:
                        seen = seen & (place <= places)
                    bias_ref[:, t * BLK : (t + 1) * BLK] = jnp.where(seen, 0.0, -1e30)
                qn = qn_ref[...]
                g = g_ref[...]
                kn = kn_ref[window, :]
                v = v_ref[window, :]
                bias = bias_ref[:, :keys]
                scores = dot(qn, kn, (1, 1)).reshape(GROUP, BLK, keys) + bias[None]
                scores = scores.reshape(GROUP * BLK, keys)
                peak = jnp.max(scores, axis=1, keepdims=True)
                raised = jnp.exp2((scores - peak) * EXP2_FACTOR)
                weights = raised * (1.0 / jnp.sum(raised, axis=1, keepdims=True))
                rounded = weights.astype(BF16)
                out = dot(rounded, v, (1, 0))
                out_ref[...] = out
                dv_ref[window, :] += dot(rounded, g, (0, 0))
                dweights = dot(g, v, (1, 1))
                delta = jnp.sum(g.astype(F32) * out, axis=1, keepdims=True)
                dscores = (weights * (dweights - delta) * FACTOR).astype(BF16)
                dq_ref[...] = dot(dscores, kn, (1, 0))
                dk_ref[window, :] += dot(dscores, qn, (0, 0))

        for h in range(GROUP):
            unit, inverse = units[h]
            local = slice(h * BLK, (h + 1) * BLK)
            y_ref[here, h * HD : (h + 1) * HD] = out_ref[local, :].astype(BF16)
            dq = dq_ref[local, :]
            back = norm_back(dq, unit, inverse, q_gain)
            y_ref[here, WIDTH + h * HD : WIDTH + (h + 1) * HD] = back.astype(BF16)
            q_sum = q_sum + fold(dq * unit)
        return q_sum

    q_sum = lax.fori_loop(0, YS, block, jnp.zeros((8, HD), F32))
    k_sum = jnp.zeros((8, HD), F32)
    for j in range(YS):
        local = slice(j * BLK, (j + 1) * BLK)
        for ref, col in ((own_ref, column), (far_ref, 1 - column)):
            place = block_rows(2 * j + col)
            unit, _ = unit_of(ref[local, k_at])
            dk = dk_ref[place, :]
            dv = dv_ref[place, :]
            k_sum = k_sum + fold(dk * unit)
            target = own_out if ref is own_ref else far_out
            target[local, k_at] = dk.astype(target.dtype)
            target[local, v_at] = dv.astype(target.dtype)
    if part > 0:
        for before, target in ((far_before, far_out), (own_before, own_out)):
            for p in range(part):
                for at in (p, PARTS + p):
                    target[:, at * HD : (at + 1) * HD] = before[:, at * HD : (at + 1) * HD]
    sums = jnp.concatenate(
        [jnp.sum(q_sum, axis=0, keepdims=True), jnp.sum(k_sum, axis=0, keepdims=True)], axis=0
    )
    if part == 0:
        gains_ref[...] = sums
    else:
        gains_ref[...] = jnp.broadcast_to((gains_before[...] + sums)[None], gains_ref.shape)
        for step in range(YS):
            rows = block_rows(ahead(step))
            for p, ref in enumerate((y_before, y_ref)):
                outs[step][:, p * WIDTH : (p + 1) * WIDTH] = ref[rows, :WIDTH]
                outs[step][:, (PARTS + p) * WIDTH : (PARTS + p + 1) * WIDTH] = ref[rows, WIDTH:]


def attend(part, lengths, both_gains, own, far, pieces, before, others):
    span = 2 * YS * BLK
    args = [lengths, both_gains, own, far, *pieces, *before]
    half = own.shape[0]
    sums = [shape(half, 2 * PARTS * HD), shape(half, 2 * PARTS * HD, F32)]
    if part == 0:
        out_shape = [shape(half, 2 * WIDTH), *sums, shape(2, HD, F32)]
    else:
        out_shape = [shape(BLK, 2 * PARTS * WIDTH)] * YS + sums
        out_shape += [jax.ShapeDtypeStruct((others, 2, HD), F32)]
    scratch = [
        pltpu.VMEM((span, HD), BF16),
        pltpu.VMEM((span, HD), BF16),
        pltpu.VMEM((span, HD), F32),
        pltpu.VMEM((span, HD), F32),
        pltpu.VMEM((WIDTH, HD), BF16),
        pltpu.VMEM((WIDTH, HD), BF16),
        pltpu.VMEM((WIDTH, HD), F32),
        pltpu.VMEM((WIDTH, HD), F32),
        pltpu.VMEM((BLK, WINDOWS * BLK), F32),
    ]
    if part > 0:
        scratch += [pltpu.VMEM((half, 2 * WIDTH), BF16)] * 2
    return pl.pallas_call(
        functools.partial(attend_kernel, part),
        out_shape=out_shape,
        in_specs=specs([pltpu.SMEM] + [VMEM] * (len(args) - 1)),
        out_specs=specs([VMEM] * len(out_shape)),
        scratch_shapes=scratch,
        compiler_params=LIMIT,
        cost_estimate=pl.CostEstimate(
            flops=10 * 2 * GROUP * half * 384 * HD, bytes_accessed=4 << 20, transcendentals=GROUP * half * 384
        ),
    )(*args)


def finish_kv_kernel(both_gains_ref, kv_ref, own_ref, far_ref, gains_ref, *refs):
    outs = refs[:YS]
    y_ref = refs[YS]
    k_gain = both_gains_ref[1:2, :]
    for p in range(PARTS):
        k_at = slice(p * HD, (p + 1) * HD)
        v_at = slice((PARTS + p) * HD, (PARTS + p + 1) * HD)
        unit, inverse = unit_of(kv_ref[:, k_at])
        dk = own_ref[:, k_at] + far_ref[:, k_at].astype(F32)
        y_ref[:, k_at] = norm_back(dk, unit, inverse, k_gain).astype(BF16)
        y_ref[:, v_at] = (own_ref[:, v_at] + far_ref[:, v_at].astype(F32)).astype(BF16)
    rest = jnp.concatenate([jnp.sum(gains_ref[...], axis=0), jnp.zeros((TAIL - 2, HD), F32)], axis=0)
    for step in range(YS):
        outs[step][:BLK, :] = y_ref[block_rows(ahead(step)), :]
        outs[step][BLK:, 3 * HD :] = jnp.zeros((TAIL, HD), BF16)
    for n in range(3):
        term = rest.astype(BF16)
        rest = rest - term.astype(F32)
        for step in range(YS):
            outs[step][BLK:, n * HD : (n + 1) * HD] = term


def unpack_moves(half, pieces, results):
    moves = []
    for step in range(YS):
        for n, result in enumerate(results):
            at = pl.ds(pl.multiple_of(behind(step) * half, half), half)
            moves.append((pieces[step].at[pl.ds(0, BLK), pl.ds(n * half, half)], result.at[:, at]))
    return moves


def unpack_qg_kernel(*refs):
    do_copies(unpack_moves(PARTS * WIDTH, refs[:YS], refs[YS:-1]), refs[-1])


def unpack_kv_kernel(scales, *refs):
    pieces = refs[:YS]
    dk_ref, dv_ref, q_ref, k_ref, sums_ref, sems = refs[YS:]
    for step in range(YS):
        tail = pieces[step][BLK:, :].astype(F32)
        whole = (tail[:, :HD] + tail[:, HD : 2 * HD]) + tail[:, 2 * HD : 3 * HD]
        sums_ref[pl.ds(behind(step), 1)] = whole[None]
    total = (sums_ref[0] + sums_ref[1]) + (sums_ref[2] + sums_ref[3])
    q_ref[...] = total[0:1] * scales[0]
    k_ref[...] = total[1:2] * scales[1]
    do_copies(unpack_moves(PARTS * HD, pieces, (dk_ref, dv_ref)), sems)


def over_y(pieces):
    moved = [pieces[0]]
    for step in range(1, YS):
        moved.append(
            lax.ppermute(
                pieces[step],
                "head",
                [(2 * y + c, 2 * ((y + step) % YS) + c) for y in range(YS) for c in range(2)],
            )
        )
    return moved


def over_x(x):
    return lax.ppermute(x, "head", [(i, i ^ 1) for i in range(2 * YS)])


def on_device(query, key_states, value_states, grad_attended, query_gain, key_gain, doc_lengths):
    replicas = lax.axis_size("dp")
    members = lax.axis_size("head")
    rows = query.shape[0]
    half = YS * rows
    wide = 2 * PARTS * HD

    pieces = pl.pallas_call(
        pack_kv_kernel,
        out_shape=[shape(rows, wide)] * YS,
        in_specs=specs([HBM] * 2),
        out_specs=specs([VMEM] * YS),
        scratch_shapes=[pltpu.SemaphoreType.DMA((2 * YS,))],
        compiler_params=PACK_LIMIT,
    )(key_states, value_states)
    kv_moved = over_y(pieces)
    soon, *pieces = pl.pallas_call(
        pack_qg_kernel,
        out_shape=[jax.ShapeDtypeStruct((YS, rows, 2 * WIDTH), BF16)] + [shape(rows, 2 * WIDTH)] * YS,
        in_specs=specs([HBM] * 2 + [VMEM]),
        out_specs=specs([VMEM] * (1 + YS)),
        scratch_shapes=[pltpu.SemaphoreType.DMA((4 * YS,))],
        compiler_params=LIMIT,
    )(query, grad_attended, kv_moved[1])
    qg_moved = over_y(pieces)
    own, both_gains = pl.pallas_call(
        gather_kv_kernel,
        out_shape=[shape(half, wide), shape(2, HD, F32)],
        in_specs=specs([VMEM] * (2 + YS)),
        out_specs=specs([VMEM] * 2),
        compiler_params=LIMIT,
    )(query_gain.reshape(1, HD), key_gain.reshape(1, HD), *kv_moved)
    far = over_x(own)
    groups = [[2 * y + c for y in range(YS)] for c in range(2)]
    soon = after(soon, both_gains)
    soon = lax.all_to_all(soon, "head", split_axis=0, concat_axis=0, tiled=True, axis_index_groups=groups)
    qg_parts = [[soon.reshape(half, 2 * WIDTH)], qg_moved]

    before = ()
    for part in range(PARTS):
        before = attend(
            part, doc_lengths, both_gains, own, far, qg_parts[part], before, 2 * replicas
        )
    *outs, far_sum, own_sum, gains = before
    far_back = over_x(far_sum)
    outs = over_y(outs)
    same_y = [[d * members + 2 * y + c for d in range(replicas) for c in range(2)] for y in range(YS)]
    gains = lax.all_to_all(
        gains, ("dp", "head"), split_axis=0, concat_axis=0, tiled=True, axis_index_groups=same_y
    )
    kv_back = pl.pallas_call(
        finish_kv_kernel,
        out_shape=[shape(rows + TAIL, wide)] * YS,
        in_specs=specs([VMEM] * 5),
        out_specs=specs([VMEM] * YS),
        scratch_shapes=[pltpu.VMEM((half, wide), BF16)],
        compiler_params=LIMIT,
    )(both_gains, own, own_sum, far_back, gains)
    kv_back = over_y(kv_back)
    out, dq = pl.pallas_call(
        unpack_qg_kernel,
        out_shape=[shape(rows, H * HD)] * 2,
        in_specs=specs([VMEM] * YS),
        out_specs=specs([HBM] * 2),
        scratch_shapes=[pltpu.SemaphoreType.DMA((2 * YS,))],
        compiler_params=LIMIT,
    )(*outs)
    all_tokens = rows * replicas * members
    scales = ((all_tokens * H) ** (-0.5), (all_tokens * KVH) ** (-0.5))
    dk, dv, q_total, k_total = pl.pallas_call(
        functools.partial(unpack_kv_kernel, scales),
        out_shape=[shape(rows, KVH * HD)] * 2 + [shape(1, HD, F32)] * 2,
        in_specs=specs([VMEM] * YS),
        out_specs=specs([HBM] * 2 + [VMEM] * 2),
        scratch_shapes=[pltpu.VMEM((YS, TAIL, HD), F32), pltpu.SemaphoreType.DMA((2 * YS,))],
        compiler_params=LIMIT,
    )(*kv_back)
    return out, dq, dk, dv, q_total.reshape(HD), k_total.reshape(HD)


def solution(mesh):
    rows = P(("dp", "head"), None)
    in_specs = (rows, rows, rows, rows, P(), P(), P())
    out_specs = (rows, rows, rows, rows, P(), P())
    return jax.shard_map(
        on_device, mesh=mesh, in_specs=in_specs, out_specs=out_specs, check_vma=False
    )
```

```python
import functools
import math

import jax
import jax.numpy as jnp
from jax import lax
from jax.experimental import pallas as pl
from jax.experimental.pallas import tpu as pltpu
from jax.sharding import PartitionSpec as P

H = 32
KVH = 8
HD = 128
GROUP = H // KVH
MOST_DOC = 512
BLK = 128
WINDOWS = MOST_DOC // BLK + 1
YS = 4
PARTS = KVH // YS
WIDTH = GROUP * HD
TAIL = 16
PAIR = 2
EPS = 1e-06
FACTOR = HD ** (-0.5)
EXP2_FACTOR = FACTOR * math.log2(math.e)
F32 = jnp.float32
BF16 = jnp.bfloat16
HBM = pltpu.HBM
VMEM = pltpu.VMEM
PACK_LIMIT = pltpu.CompilerParams(vmem_limit_bytes=60 * 1024 * 1024)
LIMIT = pltpu.CompilerParams(vmem_limit_bytes=20 * 1024 * 1024)


def dot(left, right, contract):
    return lax.dot_general(left, right, ((contract[:1], contract[1:]), ((), ())), preferred_element_type=F32)


def specs(spaces):
    return [pl.BlockSpec(memory_space=space) for space in spaces]


def shape(rows, columns, kind=BF16):
    return jax.ShapeDtypeStruct((rows, columns), kind)


def my_y():
    return lax.axis_index("head") // 2


def ahead(step):
    return lax.rem(my_y() + step, YS)


def behind(step):
    return lax.rem(my_y() + (YS - step), YS)


def block_rows(index):
    return pl.ds(pl.multiple_of(index * BLK, BLK), BLK)


def do_copies(moves, sems):
    started = [pltpu.make_async_copy(a, b, sems.at[i]) for i, (a, b) in enumerate(moves)]
    for move in started:
        move.start()
    for move in started:
        move.wait()


def pack_kv_kernel(k_ref, v_ref, *refs):
    kv, sems = refs[:YS], refs[YS]
    wide = PARTS * HD
    moves = []
    for step in range(YS):
        at = pl.ds(pl.multiple_of(ahead(step) * wide, wide), wide)
        moves.append((k_ref.at[:, at], kv[step].at[:, pl.ds(0, wide)]))
        moves.append((v_ref.at[:, at], kv[step].at[:, pl.ds(wide, wide)]))
    do_copies(moves, sems)


def pack_qg_kernel(q_ref, g_ref, _, *refs):
    soon, qg, sems = refs[0], refs[1 : 1 + YS], refs[1 + YS]
    moves = []
    for y in range(YS):
        at = pl.ds(y * (PARTS * WIDTH), WIDTH)
        moves.append((q_ref.at[:, at], soon.at[y, :, pl.ds(0, WIDTH)]))
        moves.append((g_ref.at[:, at], soon.at[y, :, pl.ds(WIDTH, WIDTH)]))
    for step in range(YS):
        at = pl.ds(pl.multiple_of(ahead(step) * (PARTS * WIDTH) + WIDTH, WIDTH), WIDTH)
        moves.append((q_ref.at[:, at], qg[step].at[:, pl.ds(0, WIDTH)]))
        moves.append((g_ref.at[:, at], qg[step].at[:, pl.ds(WIDTH, WIDTH)]))
    do_copies(moves, sems)


def after_kernel(*refs):
    pass


def after(x, first):
    return pl.pallas_call(
        after_kernel,
        out_shape=jax.ShapeDtypeStruct(x.shape, x.dtype),
        in_specs=specs([pl.ANY] * 2),
        out_specs=specs([pl.ANY])[0],
        input_output_aliases={0: 0},
    )(x, first)


def gather_kv_kernel(q_gain_ref, k_gain_ref, *refs):
    out, gains_ref = refs[YS:]
    gains_ref[0:1, :] = q_gain_ref[...]
    gains_ref[1:2, :] = k_gain_ref[...]
    for step in range(YS):
        out[block_rows(behind(step)), :] = refs[step][...]


def unit_of(raw):
    values = raw.astype(F32)
    inverse = lax.rsqrt(jnp.mean(values * values, axis=-1, keepdims=True) + EPS)
    return values * inverse, inverse


def norm_back(grad, unit, inverse, gain):
    scaled = grad * gain
    return inverse * (scaled - unit * jnp.mean(scaled * unit, axis=-1, keepdims=True))


def fold(x):
    return jnp.sum(x.reshape(x.shape[0] // 8, 8, x.shape[1]), axis=0)


def attend_kernel(part, *refs):
    refs = list(refs)
    lengths_ref, both_gains_ref, own_ref, far_ref = refs[:4]
    del refs[:4]
    if part == 0:
        qg_ref, y_ref, far_out, own_out, gains_ref = refs[:5]
        del refs[:5]
    else:
        pieces = refs[:YS]
        y_before, far_before, own_before, gains_before = refs[YS : YS + 4]
        del refs[: YS + 4]
        outs = refs[:YS]
        far_out, own_out, gains_ref = refs[YS : YS + 3]
        del refs[: YS + 3]
        qg_ref = refs.pop()
        y_ref = refs.pop()
    kn_ref, v_ref, dk_ref, dv_ref, unit_ref, inv_ref, qn_ref, g_ref, dq_ref = refs
    replica = lax.axis_index("dp")
    column = lax.rem(lax.axis_index("head"), 2)
    q_gain = both_gains_ref[0:1, :]
    k_gain = both_gains_ref[1:2, :]
    k_at = slice(part * HD, (part + 1) * HD)
    v_at = slice((PARTS + part) * HD, (PARTS + part + 1) * HD)
    for j in range(YS):
        local = slice(j * BLK, (j + 1) * BLK)
        for ref, col in ((own_ref, column), (far_ref, 1 - column)):
            place = block_rows(2 * j + col)
            unit, _ = unit_of(ref[local, k_at])
            kn_ref[place, :] = (unit * k_gain).astype(BF16)
            v_ref[place, :] = ref[local, v_at]
    if part > 0:
        for step in range(YS):
            qg_ref[block_rows(behind(step)), :] = pieces[step][...]
    dk_ref[...] = jnp.zeros_like(dk_ref)
    dv_ref[...] = jnp.zeros_like(dv_ref)
    for h in range(GROUP):
        unit, inverse = unit_of(qg_ref[:, h * HD : (h + 1) * HD])
        unit_ref[h] = unit
        inv_ref[h] = jnp.broadcast_to(inverse, unit.shape)
        normed = (unit * q_gain).astype(BF16)
        g = qg_ref[:, WIDTH + h * HD : WIDTH + (h + 1) * HD]
        for j in range(YS):
            to = slice(j * WIDTH + h * BLK, j * WIDTH + (h + 1) * BLK)
            qn_ref[to, :] = normed[j * BLK : (j + 1) * BLK]
            g_ref[to, :] = g[j * BLK : (j + 1) * BLK]
    ends = []
    total = jnp.int32(0)
    for d in range(lengths_ref.shape[1]):
        total = total + lengths_ref[replica, d]
        ends.append(total)

    def steps(count, first):
        blocks = []
        needed = jnp.int32(1)
        for n in range(count):
            j = first + n
            i = 2 * j + column
            begin0 = jnp.int32(0)
            for end in ends:
                begin0 = jnp.where(end <= i * BLK, end, begin0)
            needed = jnp.maximum(needed, i - begin0 // BLK + 1)
            blocks.append((j, i))

        def attend_window(tiles):
            keys = tiles * BLK
            rows = [pl.ds(pl.multiple_of(j * WIDTH, WIDTH), WIDTH) for j, _ in blocks]
            starts = [jnp.maximum(i - (tiles - 1), 0) * BLK for _, i in blocks]
            windows = [pl.ds(pl.multiple_of(k0, BLK), keys) for k0 in starts]
            qn = [qn_ref[at, :] for at in rows]
            g = [g_ref[at, :] for at in rows]
            kn = [kn_ref[at, :] for at in windows]
            v = [v_ref[at, :] for at in windows]
            scores = [dot(a, b, (1, 1)) for a, b in zip(qn, kn)]
            dweights = [dot(a, b, (1, 1)) for a, b in zip(g, v)]
            biases = []
            for (j, i), k0 in zip(blocks, starts):
                places = i * BLK + lax.broadcasted_iota(jnp.int32, (BLK, BLK), 0)
                begins = jnp.zeros((BLK, BLK), jnp.int32)
                for end in ends:
                    begins = jnp.where(end <= places, end, begins)
                lane = k0 + lax.broadcasted_iota(jnp.int32, (BLK, BLK), 1)
                biases.append(
                    jnp.concatenate(
                        [
                            jnp.where((lane + t * BLK >= begins) & (lane + t * BLK <= places), 0.0, -1e30)
                            for t in range(tiles)
                        ],
                        axis=1,
                    )
                )
            scores = [
                (x.reshape(GROUP, BLK, keys) + bias[None]).reshape(WIDTH, keys) for x, bias in zip(scores, biases)
            ]
            raised = [jnp.exp2((x - jnp.max(x, axis=1, keepdims=True)) * EXP2_FACTOR) for x in scores]
            weights = [x * (1.0 / jnp.sum(x, axis=1, keepdims=True)) for x in raised]
            rounded = [x.astype(BF16) for x in weights]
            out = [dot(x, b, (1, 0)) for x, b in zip(rounded, v)]
            delta = [jnp.sum(a.astype(F32) * x, axis=1, keepdims=True) for a, x in zip(g, out)]
            dscores = [
                (w * (dw - d) * FACTOR).astype(BF16) for w, dw, d in zip(weights, dweights, delta)
            ]
            for n, (j, _) in enumerate(blocks):
                dq_ref[rows[n], :] = dot(dscores[n], kn[n], (1, 0))
                dv_ref[n, windows[n], :] += dot(rounded[n], g[n], (0, 0))
                dk_ref[n, windows[n], :] += dot(dscores[n], qn[n], (0, 0))
                here = block_rows(j)
                for h in range(GROUP):
                    y_ref[here, h * HD : (h + 1) * HD] = out[n][h * BLK : (h + 1) * BLK, :].astype(BF16)

        for tiles in range(1, WINDOWS + 1):

            @pl.when(needed == tiles)
            def _():
                attend_window(tiles)

    def pair(p, carry):
        steps(PAIR, PAIR * p)
        return carry

    lax.fori_loop(0, YS // PAIR, pair, 0)
    q_sum = jnp.zeros((8, HD), F32)
    for h in range(GROUP):
        for j in range(YS):
            local = slice(j * BLK, (j + 1) * BLK)
            unit = unit_ref[h, local, :]
            dq = dq_ref[j * WIDTH + h * BLK : j * WIDTH + (h + 1) * BLK, :]
            back = norm_back(dq, unit, inv_ref[h, local, :], q_gain)
            y_ref[local, WIDTH + h * HD : WIDTH + (h + 1) * HD] = back.astype(BF16)
            q_sum = q_sum + fold(dq * unit)
    k_sum = jnp.zeros((8, HD), F32)
    for j in range(YS):
        local = slice(j * BLK, (j + 1) * BLK)
        for ref, col in ((own_ref, column), (far_ref, 1 - column)):
            place = block_rows(2 * j + col)
            unit, _ = unit_of(ref[local, k_at])
            dk = sum(dk_ref[n, place, :] for n in range(PAIR))
            dv = sum(dv_ref[n, place, :] for n in range(PAIR))
            k_sum = k_sum + fold(dk * unit)
            target = own_out if ref is own_ref else far_out
            target[local, k_at] = dk.astype(target.dtype)
            target[local, v_at] = dv.astype(target.dtype)
    if part > 0:
        for before, target in ((far_before, far_out), (own_before, own_out)):
            for p in range(part):
                for at in (p, PARTS + p):
                    target[:, at * HD : (at + 1) * HD] = before[:, at * HD : (at + 1) * HD]
    sums = jnp.concatenate(
        [jnp.sum(q_sum, axis=0, keepdims=True), jnp.sum(k_sum, axis=0, keepdims=True)], axis=0
    )
    if part == 0:
        gains_ref[...] = sums
    else:
        gains_ref[...] = jnp.broadcast_to((gains_before[...] + sums)[None], gains_ref.shape)
        for step in range(YS):
            rows = block_rows(ahead(step))
            for p, ref in enumerate((y_before, y_ref)):
                outs[step][:, p * WIDTH : (p + 1) * WIDTH] = ref[rows, :WIDTH]
                outs[step][:, (PARTS + p) * WIDTH : (PARTS + p + 1) * WIDTH] = ref[rows, WIDTH:]


def attend(part, lengths, both_gains, own, far, pieces, before, others):
    span = 2 * YS * BLK
    args = [lengths, both_gains, own, far, *pieces, *before]
    half = own.shape[0]
    sums = [shape(half, 2 * PARTS * HD), shape(half, 2 * PARTS * HD, F32)]
    if part == 0:
        out_shape = [shape(half, 2 * WIDTH), *sums, shape(2, HD, F32)]
    else:
        out_shape = [shape(BLK, 2 * PARTS * WIDTH)] * YS + sums
        out_shape += [jax.ShapeDtypeStruct((others, 2, HD), F32)]
    scratch = [
        pltpu.VMEM((span, HD), BF16),
        pltpu.VMEM((span, HD), BF16),
        pltpu.VMEM((PAIR, span, HD), F32),
        pltpu.VMEM((PAIR, span, HD), F32),
        pltpu.VMEM((GROUP, half, HD), F32),
        pltpu.VMEM((GROUP, half, HD), F32),
        pltpu.VMEM((GROUP * half, HD), BF16),
        pltpu.VMEM((GROUP * half, HD), BF16),
        pltpu.VMEM((GROUP * half, HD), F32),
    ]
    if part > 0:
        scratch += [pltpu.VMEM((half, 2 * WIDTH), BF16)] * 2
    return pl.pallas_call(
        functools.partial(attend_kernel, part),
        out_shape=out_shape,
        in_specs=specs([pltpu.SMEM] + [VMEM] * (len(args) - 1)),
        out_specs=specs([VMEM] * len(out_shape)),
        scratch_shapes=scratch,
        compiler_params=LIMIT,
        cost_estimate=pl.CostEstimate(
            flops=10 * 2 * GROUP * half * 384 * HD, bytes_accessed=4 << 20, transcendentals=GROUP * half * 384
        ),
    )(*args)


def finish_kv_kernel(both_gains_ref, kv_ref, own_ref, far_ref, gains_ref, *refs):
    outs = refs[:YS]
    y_ref = refs[YS]
    k_gain = both_gains_ref[1:2, :]
    for p in range(PARTS):
        k_at = slice(p * HD, (p + 1) * HD)
        v_at = slice((PARTS + p) * HD, (PARTS + p + 1) * HD)
        unit, inverse = unit_of(kv_ref[:, k_at])
        dk = own_ref[:, k_at] + far_ref[:, k_at].astype(F32)
        y_ref[:, k_at] = norm_back(dk, unit, inverse, k_gain).astype(BF16)
        y_ref[:, v_at] = (own_ref[:, v_at] + far_ref[:, v_at].astype(F32)).astype(BF16)
    rest = jnp.concatenate([jnp.sum(gains_ref[...], axis=0), jnp.zeros((TAIL - 2, HD), F32)], axis=0)
    for step in range(YS):
        outs[step][:BLK, :] = y_ref[block_rows(ahead(step)), :]
        outs[step][BLK:, 3 * HD :] = jnp.zeros((TAIL, HD), BF16)
    for n in range(3):
        term = rest.astype(BF16)
        rest = rest - term.astype(F32)
        for step in range(YS):
            outs[step][BLK:, n * HD : (n + 1) * HD] = term


def unpack_moves(half, pieces, results):
    moves = []
    for step in range(YS):
        for n, result in enumerate(results):
            at = pl.ds(pl.multiple_of(behind(step) * half, half), half)
            moves.append((pieces[step].at[pl.ds(0, BLK), pl.ds(n * half, half)], result.at[:, at]))
    return moves


def unpack_qg_kernel(*refs):
    do_copies(unpack_moves(PARTS * WIDTH, refs[:YS], refs[YS:-1]), refs[-1])


def unpack_kv_kernel(scales, *refs):
    pieces = refs[:YS]
    dk_ref, dv_ref, q_ref, k_ref, sums_ref, sems = refs[YS:]
    for step in range(YS):
        tail = pieces[step][BLK:, :].astype(F32)
        whole = (tail[:, :HD] + tail[:, HD : 2 * HD]) + tail[:, 2 * HD : 3 * HD]
        sums_ref[pl.ds(behind(step), 1)] = whole[None]
    total = (sums_ref[0] + sums_ref[1]) + (sums_ref[2] + sums_ref[3])
    q_ref[...] = total[0:1] * scales[0]
    k_ref[...] = total[1:2] * scales[1]
    do_copies(unpack_moves(PARTS * HD, pieces, (dk_ref, dv_ref)), sems)


def over_y(pieces):
    moved = [pieces[0]]
    for step in range(1, YS):
        moved.append(
            lax.ppermute(
                pieces[step],
                "head",
                [(2 * y + c, 2 * ((y + step) % YS) + c) for y in range(YS) for c in range(2)],
            )
        )
    return moved


def over_x(x):
    return lax.ppermute(x, "head", [(i, i ^ 1) for i in range(2 * YS)])


def on_device(query, key_states, value_states, grad_attended, query_gain, key_gain, doc_lengths):
    replicas = lax.axis_size("dp")
    members = lax.axis_size("head")
    rows = query.shape[0]
    half = YS * rows
    wide = 2 * PARTS * HD

    pieces = pl.pallas_call(
        pack_kv_kernel,
        out_shape=[shape(rows, wide)] * YS,
        in_specs=specs([HBM] * 2),
        out_specs=specs([VMEM] * YS),
        scratch_shapes=[pltpu.SemaphoreType.DMA((2 * YS,))],
        compiler_params=PACK_LIMIT,
    )(key_states, value_states)
    kv_moved = over_y(pieces)
    soon, *pieces = pl.pallas_call(
        pack_qg_kernel,
        out_shape=[jax.ShapeDtypeStruct((YS, rows, 2 * WIDTH), BF16)] + [shape(rows, 2 * WIDTH)] * YS,
        in_specs=specs([HBM] * 2 + [VMEM]),
        out_specs=specs([VMEM] * (1 + YS)),
        scratch_shapes=[pltpu.SemaphoreType.DMA((4 * YS,))],
        compiler_params=LIMIT,
    )(query, grad_attended, kv_moved[1])
    qg_moved = over_y(pieces)
    own, both_gains = pl.pallas_call(
        gather_kv_kernel,
        out_shape=[shape(half, wide), shape(2, HD, F32)],
        in_specs=specs([VMEM] * (2 + YS)),
        out_specs=specs([VMEM] * 2),
        compiler_params=LIMIT,
    )(query_gain.reshape(1, HD), key_gain.reshape(1, HD), *kv_moved)
    far = over_x(own)
    groups = [[2 * y + c for y in range(YS)] for c in range(2)]
    soon = after(soon, both_gains)
    soon = lax.all_to_all(soon, "head", split_axis=0, concat_axis=0, tiled=True, axis_index_groups=groups)
    qg_parts = [[soon.reshape(half, 2 * WIDTH)], qg_moved]

    before = ()
    for part in range(PARTS):
        before = attend(
            part, doc_lengths, both_gains, own, far, qg_parts[part], before, 2 * replicas
        )
    *outs, far_sum, own_sum, gains = before
    far_back = over_x(far_sum)
    outs = over_y(outs)
    same_y = [[d * members + 2 * y + c for d in range(replicas) for c in range(2)] for y in range(YS)]
    gains = lax.all_to_all(
        gains, ("dp", "head"), split_axis=0, concat_axis=0, tiled=True, axis_index_groups=same_y
    )
    kv_back = pl.pallas_call(
        finish_kv_kernel,
        out_shape=[shape(rows + TAIL, wide)] * YS,
        in_specs=specs([VMEM] * 5),
        out_specs=specs([VMEM] * YS),
        scratch_shapes=[pltpu.VMEM((half, wide), BF16)],
        compiler_params=LIMIT,
    )(both_gains, own, own_sum, far_back, gains)
    kv_back = over_y(kv_back)
    out, dq = pl.pallas_call(
        unpack_qg_kernel,
        out_shape=[shape(rows, H * HD)] * 2,
        in_specs=specs([VMEM] * YS),
        out_specs=specs([HBM] * 2),
        scratch_shapes=[pltpu.SemaphoreType.DMA((2 * YS,))],
        compiler_params=LIMIT,
    )(*outs)
    all_tokens = rows * replicas * members
    scales = ((all_tokens * H) ** (-0.5), (all_tokens * KVH) ** (-0.5))
    dk, dv, q_total, k_total = pl.pallas_call(
        functools.partial(unpack_kv_kernel, scales),
        out_shape=[shape(rows, KVH * HD)] * 2 + [shape(1, HD, F32)] * 2,
        in_specs=specs([VMEM] * YS),
        out_specs=specs([HBM] * 2 + [VMEM] * 2),
        scratch_shapes=[pltpu.VMEM((YS, TAIL, HD), F32), pltpu.SemaphoreType.DMA((2 * YS,))],
        compiler_params=LIMIT,
    )(*kv_back)
    return out, dq, dk, dv, q_total.reshape(HD), k_total.reshape(HD)


def solution(mesh):
    rows = P(("dp", "head"), None)
    in_specs = (rows, rows, rows, rows, P(), P(), P())
    out_specs = (rows, rows, rows, rows, P(), P())
    return jax.shard_map(
        on_device, mesh=mesh, in_specs=in_specs, out_specs=out_specs, check_vma=False
    )
```

```python
import functools
import math

import jax
import jax.numpy as jnp
from jax import lax
from jax.experimental import pallas as pl
from jax.experimental.pallas import tpu as pltpu
from jax.sharding import PartitionSpec as P

H = 32
KVH = 8
HD = 128
GROUP = H // KVH
MOST_DOC = 512
BLK = 128
WINDOWS = MOST_DOC // BLK + 1
YS = 4
PARTS = KVH // YS
WIDTH = GROUP * HD
TAIL = 16
PAIR = 2
EPS = 1e-06
FACTOR = HD ** (-0.5)
EXP2_FACTOR = FACTOR * math.log2(math.e)
F32 = jnp.float32
BF16 = jnp.bfloat16
HBM = pltpu.HBM
VMEM = pltpu.VMEM
PACK_LIMIT = pltpu.CompilerParams(vmem_limit_bytes=60 * 1024 * 1024)
LIMIT = pltpu.CompilerParams(vmem_limit_bytes=20 * 1024 * 1024)


def dot(left, right, contract):
    return lax.dot_general(left, right, ((contract[:1], contract[1:]), ((), ())), preferred_element_type=F32)


def specs(spaces):
    return [pl.BlockSpec(memory_space=space) for space in spaces]


def shape(rows, columns, kind=BF16):
    return jax.ShapeDtypeStruct((rows, columns), kind)


def my_y():
    return lax.axis_index("head") // 2


def ahead(step):
    return lax.rem(my_y() + step, YS)


def behind(step):
    return lax.rem(my_y() + (YS - step), YS)


def block_rows(index):
    return pl.ds(pl.multiple_of(index * BLK, BLK), BLK)


def do_copies(moves, sems):
    started = [pltpu.make_async_copy(a, b, sems.at[i]) for i, (a, b) in enumerate(moves)]
    for move in started:
        move.start()
    for move in started:
        move.wait()


def pack_kv_kernel(k_ref, v_ref, *refs):
    kv, sems = refs[:YS], refs[YS]
    wide = PARTS * HD
    moves = []
    for step in range(YS):
        at = pl.ds(pl.multiple_of(ahead(step) * wide, wide), wide)
        moves.append((k_ref.at[:, at], kv[step].at[:, pl.ds(0, wide)]))
        moves.append((v_ref.at[:, at], kv[step].at[:, pl.ds(wide, wide)]))
    do_copies(moves, sems)


def pack_qg_kernel(q_ref, g_ref, _, *refs):
    soon, qg, sems = refs[0], refs[1 : 1 + YS], refs[1 + YS]
    moves = []
    for y in range(YS):
        at = pl.ds(y * (PARTS * WIDTH), WIDTH)
        moves.append((q_ref.at[:, at], soon.at[y, :, pl.ds(0, WIDTH)]))
        moves.append((g_ref.at[:, at], soon.at[y, :, pl.ds(WIDTH, WIDTH)]))
    for step in range(YS):
        at = pl.ds(pl.multiple_of(ahead(step) * (PARTS * WIDTH) + WIDTH, WIDTH), WIDTH)
        moves.append((q_ref.at[:, at], qg[step].at[:, pl.ds(0, WIDTH)]))
        moves.append((g_ref.at[:, at], qg[step].at[:, pl.ds(WIDTH, WIDTH)]))
    do_copies(moves, sems)


def after_kernel(*refs):
    pass


def after(x, first):
    return pl.pallas_call(
        after_kernel,
        out_shape=jax.ShapeDtypeStruct(x.shape, x.dtype),
        in_specs=specs([pl.ANY] * 2),
        out_specs=specs([pl.ANY])[0],
        input_output_aliases={0: 0},
    )(x, first)


def gather_kv_kernel(q_gain_ref, k_gain_ref, *refs):
    out, gains_ref = refs[YS:]
    gains_ref[0:1, :] = q_gain_ref[...]
    gains_ref[1:2, :] = k_gain_ref[...]
    for step in range(YS):
        out[block_rows(behind(step)), :] = refs[step][...]


def unit_of(raw):
    values = raw.astype(F32)
    inverse = lax.rsqrt(jnp.mean(values * values, axis=-1, keepdims=True) + EPS)
    return values * inverse, inverse


def norm_back(grad, unit, inverse, gain):
    scaled = grad * gain
    return inverse * (scaled - unit * jnp.mean(scaled * unit, axis=-1, keepdims=True))


def fold(x):
    return jnp.sum(x.reshape(x.shape[0] // 8, 8, x.shape[1]), axis=0)


def attend_kernel(part, *refs):
    refs = list(refs)
    lengths_ref, both_gains_ref, own_ref, far_ref = refs[:4]
    del refs[:4]
    if part == 0:
        qg_ref = refs.pop(0)
        arrived = [(j, qg_ref.at[j * BLK : (j + 1) * BLK]) for j in range(YS)]
    else:
        arrived = [(behind(step), refs[step]) for step in range(YS)]
        y_before = refs[YS : 2 * YS]
        far_before, own_before, gains_before = refs[2 * YS : 2 * YS + 3]
        del refs[: 2 * YS + 3]
    outs = refs[:YS]
    far_out, own_out, gains_ref = refs[YS : YS + 3]
    kn_ref, v_ref, dk_ref, dv_ref, unit_ref, inv_ref, qn_ref, g_ref, dq_ref, out_ref = refs[YS + 3 :]
    replica = lax.axis_index("dp")
    column = lax.rem(lax.axis_index("head"), 2)
    q_gain = both_gains_ref[0:1, :]
    k_gain = both_gains_ref[1:2, :]
    k_at = slice(part * HD, (part + 1) * HD)
    v_at = slice((PARTS + part) * HD, (PARTS + part + 1) * HD)
    for j in range(YS):
        local = slice(j * BLK, (j + 1) * BLK)
        for ref, col in ((own_ref, column), (far_ref, 1 - column)):
            place = block_rows(2 * j + col)
            unit, _ = unit_of(ref[local, k_at])
            kn_ref[place, :] = (unit * k_gain).astype(BF16)
            v_ref[place, :] = ref[local, v_at]
    dk_ref[...] = jnp.zeros_like(dk_ref)
    dv_ref[...] = jnp.zeros_like(dv_ref)
    for j, piece in arrived:
        for h in range(GROUP):
            to = block_rows(j * GROUP + h)
            unit, inverse = unit_of(piece[:, h * HD : (h + 1) * HD])
            unit_ref[to, :] = unit
            inv_ref[to, :] = jnp.broadcast_to(inverse, unit.shape)
            qn_ref[to, :] = (unit * q_gain).astype(BF16)
            g_ref[to, :] = piece[:, WIDTH + h * HD : WIDTH + (h + 1) * HD]
    ends = []
    total = jnp.int32(0)
    for d in range(lengths_ref.shape[1]):
        total = total + lengths_ref[replica, d]
        ends.append(total)

    def steps(count, first):
        blocks = []
        needed = jnp.int32(1)
        for n in range(count):
            j = first + n
            i = 2 * j + column
            begin0 = jnp.int32(0)
            for end in ends:
                begin0 = jnp.where(end <= i * BLK, end, begin0)
            needed = jnp.maximum(needed, i - begin0 // BLK + 1)
            blocks.append((j, i))

        def attend_window(tiles):
            keys = tiles * BLK
            rows = [pl.ds(pl.multiple_of(j * WIDTH, WIDTH), WIDTH) for j, _ in blocks]
            starts = [jnp.maximum(i - (tiles - 1), 0) * BLK for _, i in blocks]
            windows = [pl.ds(pl.multiple_of(k0, BLK), keys) for k0 in starts]
            qn = [qn_ref[at, :] for at in rows]
            g = [g_ref[at, :] for at in rows]
            kn = [kn_ref[at, :] for at in windows]
            v = [v_ref[at, :] for at in windows]
            scores = [dot(a, b, (1, 1)) for a, b in zip(qn, kn)]
            dweights = [dot(a, b, (1, 1)) for a, b in zip(g, v)]
            biases = []
            for (j, i), k0 in zip(blocks, starts):
                places = i * BLK + lax.broadcasted_iota(jnp.int32, (BLK, BLK), 0)
                begins = jnp.zeros((BLK, BLK), jnp.int32)
                for end in ends:
                    begins = jnp.where(end <= places, end, begins)
                lane = k0 + lax.broadcasted_iota(jnp.int32, (BLK, BLK), 1)
                biases.append(
                    jnp.concatenate(
                        [
                            jnp.where((lane + t * BLK >= begins) & (lane + t * BLK <= places), 0.0, -1e30)
                            for t in range(tiles)
                        ],
                        axis=1,
                    )
                )
            scores = [
                (x.reshape(GROUP, BLK, keys) + bias[None]).reshape(WIDTH, keys) for x, bias in zip(scores, biases)
            ]
            raised = [jnp.exp2((x - jnp.max(x, axis=1, keepdims=True)) * EXP2_FACTOR) for x in scores]
            weights = [x * (1.0 / jnp.sum(x, axis=1, keepdims=True)) for x in raised]
            rounded = [x.astype(BF16) for x in weights]
            out = [dot(x, b, (1, 0)) for x, b in zip(rounded, v)]
            delta = [jnp.sum(a.astype(F32) * x, axis=1, keepdims=True) for a, x in zip(g, out)]
            dscores = [
                (w * (dw - d) * FACTOR).astype(BF16) for w, dw, d in zip(weights, dweights, delta)
            ]
            for n in range(len(blocks)):
                dq_ref[rows[n], :] = dot(dscores[n], kn[n], (1, 0))
                dv_ref[n, windows[n], :] += dot(rounded[n], g[n], (0, 0))
                dk_ref[n, windows[n], :] += dot(dscores[n], qn[n], (0, 0))
                out_ref[rows[n], :] = out[n].astype(BF16)

        for tiles in range(1, WINDOWS + 1):

            @pl.when(needed == tiles)
            def _():
                attend_window(tiles)

    def pair(p, carry):
        steps(PAIR, PAIR * p)
        return carry

    lax.fori_loop(0, YS // PAIR, pair, 0)
    q_sum = jnp.zeros((8, HD), F32)
    for step in range(YS):
        for h in range(GROUP):
            turn = block_rows(ahead(step) * GROUP + h)
            unit = unit_ref[turn, :]
            dq = dq_ref[turn, :]
            back = norm_back(dq, unit, inv_ref[turn, :], q_gain)
            first = part * WIDTH + h * HD
            outs[step][:, first : first + HD] = out_ref[turn, :]
            first += (part + 1) * WIDTH
            outs[step][:, first : first + HD] = back.astype(BF16)
            q_sum = q_sum + fold(dq * unit)
    k_sum = jnp.zeros((8, HD), F32)
    for j in range(YS):
        local = slice(j * BLK, (j + 1) * BLK)
        for ref, col in ((own_ref, column), (far_ref, 1 - column)):
            place = block_rows(2 * j + col)
            unit, _ = unit_of(ref[local, k_at])
            dk = sum(dk_ref[n, place, :] for n in range(PAIR))
            dv = sum(dv_ref[n, place, :] for n in range(PAIR))
            k_sum = k_sum + fold(dk * unit)
            target = own_out if ref is own_ref else far_out
            target[local, k_at] = dk.astype(target.dtype)
            target[local, v_at] = dv.astype(target.dtype)
    if part > 0:
        for before, target in ((far_before, far_out), (own_before, own_out)):
            for p in range(part):
                for at in (p, PARTS + p):
                    target[:, at * HD : (at + 1) * HD] = before[:, at * HD : (at + 1) * HD]
    sums = jnp.concatenate(
        [jnp.sum(q_sum, axis=0, keepdims=True), jnp.sum(k_sum, axis=0, keepdims=True)], axis=0
    )
    if part == 0:
        gains_ref[...] = sums
    else:
        gains_ref[...] = jnp.broadcast_to((gains_before[...] + sums)[None], gains_ref.shape)
        for step in range(YS):
            outs[step][:, :WIDTH] = y_before[step][:, :WIDTH]
            outs[step][:, PARTS * WIDTH : (PARTS + 1) * WIDTH] = y_before[step][:, WIDTH:]


def attend(part, lengths, both_gains, own, far, pieces, before, others):
    span = 2 * YS * BLK
    args = [lengths, both_gains, own, far, *pieces, *before]
    half = own.shape[0]
    sums = [shape(half, 2 * PARTS * HD), shape(half, 2 * PARTS * HD, F32)]
    if part == 0:
        out_shape = [shape(BLK, 2 * WIDTH)] * YS + [*sums, shape(2, HD, F32)]
    else:
        out_shape = [shape(BLK, 2 * PARTS * WIDTH)] * YS + sums
        out_shape += [jax.ShapeDtypeStruct((others, 2, HD), F32)]
    scratch = [
        pltpu.VMEM((span, HD), BF16),
        pltpu.VMEM((span, HD), BF16),
        pltpu.VMEM((PAIR, span, HD), F32),
        pltpu.VMEM((PAIR, span, HD), F32),
        pltpu.VMEM((GROUP * half, HD), F32),
        pltpu.VMEM((GROUP * half, HD), F32),
        pltpu.VMEM((GROUP * half, HD), BF16),
        pltpu.VMEM((GROUP * half, HD), BF16),
        pltpu.VMEM((GROUP * half, HD), F32),
    ]
    scratch += [pltpu.VMEM((GROUP * half, HD), BF16)]
    return pl.pallas_call(
        functools.partial(attend_kernel, part),
        out_shape=out_shape,
        in_specs=specs([pltpu.SMEM] + [VMEM] * (len(args) - 1)),
        out_specs=specs([VMEM] * len(out_shape)),
        scratch_shapes=scratch,
        compiler_params=LIMIT,
        cost_estimate=pl.CostEstimate(
            flops=10 * 2 * GROUP * half * 384 * HD, bytes_accessed=4 << 20, transcendentals=GROUP * half * 384
        ),
    )(*args)


def finish_kv_kernel(both_gains_ref, kv_ref, own_ref, far_ref, gains_ref, *refs):
    outs = refs[:YS]
    y_ref = refs[YS]
    k_gain = both_gains_ref[1:2, :]
    for p in range(PARTS):
        k_at = slice(p * HD, (p + 1) * HD)
        v_at = slice((PARTS + p) * HD, (PARTS + p + 1) * HD)
        unit, inverse = unit_of(kv_ref[:, k_at])
        dk = own_ref[:, k_at] + far_ref[:, k_at].astype(F32)
        y_ref[:, k_at] = norm_back(dk, unit, inverse, k_gain).astype(BF16)
        y_ref[:, v_at] = (own_ref[:, v_at] + far_ref[:, v_at].astype(F32)).astype(BF16)
    rest = jnp.concatenate([jnp.sum(gains_ref[...], axis=0), jnp.zeros((TAIL - 2, HD), F32)], axis=0)
    for step in range(YS):
        outs[step][:BLK, :] = y_ref[block_rows(ahead(step)), :]
        outs[step][BLK:, 3 * HD :] = jnp.zeros((TAIL, HD), BF16)
    for n in range(3):
        term = rest.astype(BF16)
        rest = rest - term.astype(F32)
        for step in range(YS):
            outs[step][BLK:, n * HD : (n + 1) * HD] = term


def unpack_moves(half, pieces, results):
    moves = []
    for step in range(YS):
        for n, result in enumerate(results):
            at = pl.ds(pl.multiple_of(behind(step) * half, half), half)
            moves.append((pieces[step].at[pl.ds(0, BLK), pl.ds(n * half, half)], result.at[:, at]))
    return moves


def unpack_qg_kernel(*refs):
    do_copies(unpack_moves(PARTS * WIDTH, refs[:YS], refs[YS:-1]), refs[-1])


def unpack_kv_kernel(scales, *refs):
    pieces = refs[:YS]
    dk_ref, dv_ref, q_ref, k_ref, sums_ref, sems = refs[YS:]
    for step in range(YS):
        tail = pieces[step][BLK:, :].astype(F32)
        whole = (tail[:, :HD] + tail[:, HD : 2 * HD]) + tail[:, 2 * HD : 3 * HD]
        sums_ref[pl.ds(behind(step), 1)] = whole[None]
    total = (sums_ref[0] + sums_ref[1]) + (sums_ref[2] + sums_ref[3])
    q_ref[...] = total[0:1] * scales[0]
    k_ref[...] = total[1:2] * scales[1]
    do_copies(unpack_moves(PARTS * HD, pieces, (dk_ref, dv_ref)), sems)


def over_y(pieces):
    moved = [pieces[0]]
    for step in range(1, YS):
        moved.append(
            lax.ppermute(
                pieces[step],
                "head",
                [(2 * y + c, 2 * ((y + step) % YS) + c) for y in range(YS) for c in range(2)],
            )
        )
    return moved


def over_x(x):
    return lax.ppermute(x, "head", [(i, i ^ 1) for i in range(2 * YS)])


def on_device(query, key_states, value_states, grad_attended, query_gain, key_gain, doc_lengths):
    replicas = lax.axis_size("dp")
    members = lax.axis_size("head")
    rows = query.shape[0]
    half = YS * rows
    wide = 2 * PARTS * HD

    pieces = pl.pallas_call(
        pack_kv_kernel,
        out_shape=[shape(rows, wide)] * YS,
        in_specs=specs([HBM] * 2),
        out_specs=specs([VMEM] * YS),
        scratch_shapes=[pltpu.SemaphoreType.DMA((2 * YS,))],
        compiler_params=PACK_LIMIT,
    )(key_states, value_states)
    kv_moved = over_y(pieces)
    soon, *pieces = pl.pallas_call(
        pack_qg_kernel,
        out_shape=[jax.ShapeDtypeStruct((YS, rows, 2 * WIDTH), BF16)] + [shape(rows, 2 * WIDTH)] * YS,
        in_specs=specs([HBM] * 2 + [VMEM]),
        out_specs=specs([VMEM] * (1 + YS)),
        scratch_shapes=[pltpu.SemaphoreType.DMA((4 * YS,))],
        compiler_params=LIMIT,
    )(query, grad_attended, kv_moved[1])
    qg_moved = over_y(pieces)
    own, both_gains = pl.pallas_call(
        gather_kv_kernel,
        out_shape=[shape(half, wide), shape(2, HD, F32)],
        in_specs=specs([VMEM] * (2 + YS)),
        out_specs=specs([VMEM] * 2),
        compiler_params=LIMIT,
    )(query_gain.reshape(1, HD), key_gain.reshape(1, HD), *kv_moved)
    far = over_x(own)
    groups = [[2 * y + c for y in range(YS)] for c in range(2)]
    soon = after(soon, both_gains)
    soon = lax.all_to_all(soon, "head", split_axis=0, concat_axis=0, tiled=True, axis_index_groups=groups)
    qg_parts = [[soon.reshape(half, 2 * WIDTH)], qg_moved]

    before = ()
    for part in range(PARTS):
        before = attend(
            part, doc_lengths, both_gains, own, far, qg_parts[part], before, 2 * replicas
        )
    *outs, far_sum, own_sum, gains = before
    far_back = over_x(far_sum)
    outs = over_y(outs)
    same_y = [[d * members + 2 * y + c for d in range(replicas) for c in range(2)] for y in range(YS)]
    gains = lax.all_to_all(
        gains, ("dp", "head"), split_axis=0, concat_axis=0, tiled=True, axis_index_groups=same_y
    )
    kv_back = pl.pallas_call(
        finish_kv_kernel,
        out_shape=[shape(rows + TAIL, wide)] * YS,
        in_specs=specs([VMEM] * 5),
        out_specs=specs([VMEM] * YS),
        scratch_shapes=[pltpu.VMEM((half, wide), BF16)],
        compiler_params=LIMIT,
    )(both_gains, own, own_sum, far_back, gains)
    kv_back = over_y(kv_back)
    out, dq = pl.pallas_call(
        unpack_qg_kernel,
        out_shape=[shape(rows, H * HD)] * 2,
        in_specs=specs([VMEM] * YS),
        out_specs=specs([HBM] * 2),
        scratch_shapes=[pltpu.SemaphoreType.DMA((2 * YS,))],
        compiler_params=LIMIT,
    )(*outs)
    all_tokens = rows * replicas * members
    scales = ((all_tokens * H) ** (-0.5), (all_tokens * KVH) ** (-0.5))
    dk, dv, q_total, k_total = pl.pallas_call(
        functools.partial(unpack_kv_kernel, scales),
        out_shape=[shape(rows, KVH * HD)] * 2 + [shape(1, HD, F32)] * 2,
        in_specs=specs([VMEM] * YS),
        out_specs=specs([HBM] * 2 + [VMEM] * 2),
        scratch_shapes=[pltpu.VMEM((YS, TAIL, HD), F32), pltpu.SemaphoreType.DMA((2 * YS,))],
        compiler_params=LIMIT,
    )(*kv_back)
    return out, dq, dk, dv, q_total.reshape(HD), k_total.reshape(HD)


def solution(mesh):
    rows = P(("dp", "head"), None)
    in_specs = (rows, rows, rows, rows, P(), P(), P())
    out_specs = (rows, rows, rows, rows, P(), P())
    return jax.shard_map(
        on_device, mesh=mesh, in_specs=in_specs, out_specs=out_specs, check_vma=False
    )
```

```python
import functools
import math

import jax
import jax.numpy as jnp
from jax import lax
from jax.experimental import pallas as pl
from jax.experimental.pallas import tpu as pltpu
from jax.sharding import PartitionSpec as P

H = 32
KVH = 8
HD = 128
GROUP = H // KVH
MOST_DOC = 512
BLK = 128
WINDOWS = MOST_DOC // BLK + 1
YS = 4
PARTS = KVH // YS
WIDTH = GROUP * HD
TAIL = 16
PAIR = 2
EPS = 1e-06
FACTOR = HD ** (-0.5)
EXP2_FACTOR = FACTOR * math.log2(math.e)
F32 = jnp.float32
BF16 = jnp.bfloat16
HBM = pltpu.HBM
VMEM = pltpu.VMEM
PACK_LIMIT = pltpu.CompilerParams(vmem_limit_bytes=60 * 1024 * 1024)
LIMIT = pltpu.CompilerParams(vmem_limit_bytes=20 * 1024 * 1024)


def dot(left, right, contract):
    return lax.dot_general(left, right, ((contract[:1], contract[1:]), ((), ())), preferred_element_type=F32)


def specs(spaces):
    return [pl.BlockSpec(memory_space=space) for space in spaces]


def shape(rows, columns, kind=BF16):
    return jax.ShapeDtypeStruct((rows, columns), kind)


def my_y():
    return lax.axis_index("head") // 2


def ahead(step):
    return lax.rem(my_y() + step, YS)


def behind(step):
    return lax.rem(my_y() + (YS - step), YS)


def block_rows(index):
    return pl.ds(pl.multiple_of(index * BLK, BLK), BLK)


def start_copies(moves, sems):
    started = [pltpu.make_async_copy(a, b, sems.at[i]) for i, (a, b) in enumerate(moves)]
    for move in started:
        move.start()
    return started


def do_copies(moves, sems):
    for move in start_copies(moves, sems):
        move.wait()


def pack_kv_kernel(k_ref, v_ref, *refs):
    kv, sems = refs[:YS], refs[YS]
    wide = PARTS * HD
    moves = []
    for step in range(YS):
        at = pl.ds(pl.multiple_of(ahead(step) * wide, wide), wide)
        moves.append((k_ref.at[:, at], kv[step].at[:, pl.ds(0, wide)]))
        moves.append((v_ref.at[:, at], kv[step].at[:, pl.ds(wide, wide)]))
    do_copies(moves, sems)


def pack_qg_kernel(q_ref, g_ref, _, *refs):
    soon, qg, sems = refs[0], refs[1 : 1 + YS], refs[1 + YS]
    moves = []
    for y in range(YS):
        at = pl.ds(y * (PARTS * WIDTH), WIDTH)
        moves.append((q_ref.at[:, at], soon.at[y, :, pl.ds(0, WIDTH)]))
        moves.append((g_ref.at[:, at], soon.at[y, :, pl.ds(WIDTH, WIDTH)]))
    for step in range(YS):
        at = pl.ds(pl.multiple_of(ahead(step) * (PARTS * WIDTH) + WIDTH, WIDTH), WIDTH)
        moves.append((q_ref.at[:, at], qg[step].at[:, pl.ds(0, WIDTH)]))
        moves.append((g_ref.at[:, at], qg[step].at[:, pl.ds(WIDTH, WIDTH)]))
    do_copies(moves, sems)


def after_kernel(*refs):
    pass


def after(x, first):
    return pl.pallas_call(
        after_kernel,
        out_shape=jax.ShapeDtypeStruct(x.shape, x.dtype),
        in_specs=specs([pl.ANY] * 2),
        out_specs=specs([pl.ANY])[0],
        input_output_aliases={0: 0},
    )(x, first)


def gather_kv_kernel(q_gain_ref, k_gain_ref, *refs):
    out, gains_ref = refs[YS:]
    gains_ref[0:1, :] = q_gain_ref[...]
    gains_ref[1:2, :] = k_gain_ref[...]
    for step in range(YS):
        out[block_rows(behind(step)), :] = refs[step][...]


def unit_of(raw):
    values = raw.astype(F32)
    inverse = lax.rsqrt(jnp.mean(values * values, axis=-1, keepdims=True) + EPS)
    return values * inverse, inverse


def norm_back(grad, unit, inverse, gain):
    scaled = grad * gain
    return inverse * (scaled - unit * jnp.mean(scaled * unit, axis=-1, keepdims=True))


def fold(x):
    return jnp.sum(x.reshape(x.shape[0] // 8, 8, x.shape[1]), axis=0)


def attend_kernel(part, *refs):
    refs = list(refs)
    lengths_ref, both_gains_ref, own_ref, far_ref = refs[:4]
    del refs[:4]
    if part == 0:
        qg_ref = refs.pop(0)
        arrived = [(j, qg_ref.at[j * BLK : (j + 1) * BLK]) for j in range(YS)]
    else:
        arrived = [(behind(step), refs[step]) for step in range(YS)]
        y_before = refs[YS : 2 * YS]
        far_before, gains_before = refs[2 * YS : 2 * YS + 2]
        del refs[: 2 * YS + 2]
    outs = refs[:YS]
    far_out, own_out, gains_ref = refs[YS : YS + 3]
    kn_ref, v_ref, dk_ref, dv_ref, unit_ref, inv_ref, qn_ref, g_ref, dq_ref, out_ref = refs[YS + 3 :]
    replica = lax.axis_index("dp")
    column = lax.rem(lax.axis_index("head"), 2)
    q_gain = both_gains_ref[0:1, :]
    k_gain = both_gains_ref[1:2, :]
    k_at = slice(part * HD, (part + 1) * HD)
    v_at = slice((PARTS + part) * HD, (PARTS + part + 1) * HD)
    for j in range(YS):
        local = slice(j * BLK, (j + 1) * BLK)
        for ref, col in ((own_ref, column), (far_ref, 1 - column)):
            place = block_rows(2 * j + col)
            unit, _ = unit_of(ref[local, k_at])
            kn_ref[place, :] = (unit * k_gain).astype(BF16)
            v_ref[place, :] = ref[local, v_at]
    dk_ref[...] = jnp.zeros_like(dk_ref)
    dv_ref[...] = jnp.zeros_like(dv_ref)
    for j, piece in arrived:
        for h in range(GROUP):
            to = block_rows(j * GROUP + h)
            unit, inverse = unit_of(piece[:, h * HD : (h + 1) * HD])
            unit_ref[to, :] = unit
            inv_ref[to, :] = jnp.broadcast_to(inverse, unit.shape)
            qn_ref[to, :] = (unit * q_gain).astype(BF16)
            g_ref[to, :] = piece[:, WIDTH + h * HD : WIDTH + (h + 1) * HD]
    ends = []
    total = jnp.int32(0)
    for d in range(lengths_ref.shape[1]):
        total = total + lengths_ref[replica, d]
        ends.append(total)

    def steps(count, first):
        blocks = []
        needed = jnp.int32(1)
        for n in range(count):
            j = first + n
            i = 2 * j + column
            begin0 = jnp.int32(0)
            for end in ends:
                begin0 = jnp.where(end <= i * BLK, end, begin0)
            needed = jnp.maximum(needed, i - begin0 // BLK + 1)
            blocks.append((j, i))

        def attend_window(tiles):
            keys = tiles * BLK
            rows = [pl.ds(pl.multiple_of(j * WIDTH, WIDTH), WIDTH) for j, _ in blocks]
            starts = [jnp.maximum(i - (tiles - 1), 0) * BLK for _, i in blocks]
            windows = [pl.ds(pl.multiple_of(k0, BLK), keys) for k0 in starts]
            qn = [qn_ref[at, :] for at in rows]
            g = [g_ref[at, :] for at in rows]
            kn = [kn_ref[at, :] for at in windows]
            v = [v_ref[at, :] for at in windows]
            scores = [dot(a, b, (1, 1)) for a, b in zip(qn, kn)]
            dweights = [dot(a, b, (1, 1)) for a, b in zip(g, v)]
            biases = []
            for (j, i), k0 in zip(blocks, starts):
                places = i * BLK + lax.broadcasted_iota(jnp.int32, (BLK, BLK), 0)
                begins = jnp.zeros((BLK, BLK), jnp.int32)
                for end in ends:
                    begins = jnp.where(end <= places, end, begins)
                lane = k0 + lax.broadcasted_iota(jnp.int32, (BLK, BLK), 1)
                biases.append(
                    jnp.concatenate(
                        [
                            jnp.where((lane + t * BLK >= begins) & (lane + t * BLK <= places), 0.0, -1e30)
                            for t in range(tiles)
                        ],
                        axis=1,
                    )
                )
            scores = [
                (x.reshape(GROUP, BLK, keys) + bias[None]).reshape(WIDTH, keys) for x, bias in zip(scores, biases)
            ]
            raised = [jnp.exp2((x - jnp.max(x, axis=1, keepdims=True)) * EXP2_FACTOR) for x in scores]
            weights = [x * (1.0 / jnp.sum(x, axis=1, keepdims=True)) for x in raised]
            rounded = [x.astype(BF16) for x in weights]
            out = [dot(x, b, (1, 0)) for x, b in zip(rounded, v)]
            delta = [jnp.sum(a.astype(F32) * x, axis=1, keepdims=True) for a, x in zip(g, out)]
            dscores = [
                (w * (dw - d) * FACTOR).astype(BF16) for w, dw, d in zip(weights, dweights, delta)
            ]
            for n in range(len(blocks)):
                dq_ref[rows[n], :] = dot(dscores[n], kn[n], (1, 0))
                dv_ref[n, windows[n], :] += dot(rounded[n], g[n], (0, 0))
                dk_ref[n, windows[n], :] += dot(dscores[n], qn[n], (0, 0))
                out_ref[rows[n], :] = out[n].astype(BF16)

        for tiles in range(1, WINDOWS + 1):

            @pl.when(needed == tiles)
            def _():
                attend_window(tiles)

    def pair(p, carry):
        steps(PAIR, PAIR * p)
        return carry

    lax.fori_loop(0, YS // PAIR, pair, 0)
    q_sum = jnp.zeros((8, HD), F32)
    for step in range(YS):
        for h in range(GROUP):
            turn = block_rows(ahead(step) * GROUP + h)
            unit = unit_ref[turn, :]
            dq = dq_ref[turn, :]
            back = norm_back(dq, unit, inv_ref[turn, :], q_gain)
            first = part * WIDTH + h * HD
            outs[step][:, first : first + HD] = out_ref[turn, :]
            first += (part + 1) * WIDTH
            outs[step][:, first : first + HD] = back.astype(BF16)
            q_sum = q_sum + fold(dq * unit)
    k_sum = jnp.zeros((8, HD), F32)
    for j in range(YS):
        local = slice(j * BLK, (j + 1) * BLK)
        for ref, col in ((own_ref, column), (far_ref, 1 - column)):
            place = block_rows(2 * j + col)
            unit, _ = unit_of(ref[local, k_at])
            dk = sum(dk_ref[n, place, :] for n in range(PAIR))
            dv = sum(dv_ref[n, place, :] for n in range(PAIR))
            k_sum = k_sum + fold(dk * unit)
            if ref is own_ref:
                own_out[local, :HD] = dk
                own_out[local, HD:] = dv
            else:
                far_out[local, k_at] = dk.astype(BF16)
                far_out[local, v_at] = dv.astype(BF16)
    if part > 0:
        for at in range(0, 2 * PARTS, PARTS):
            far_out[:, at * HD : (at + 1) * HD] = far_before[:, at * HD : (at + 1) * HD]
    sums = jnp.concatenate(
        [jnp.sum(q_sum, axis=0, keepdims=True), jnp.sum(k_sum, axis=0, keepdims=True)], axis=0
    )
    if part == 0:
        gains_ref[...] = sums
    else:
        gains_ref[...] = jnp.broadcast_to((gains_before[...] + sums)[None], gains_ref.shape)
        for step in range(YS):
            outs[step][:, :WIDTH] = y_before[step][:, :WIDTH]
            outs[step][:, PARTS * WIDTH : (PARTS + 1) * WIDTH] = y_before[step][:, WIDTH:]


def attend(part, lengths, both_gains, own, far, pieces, before, others):
    span = 2 * YS * BLK
    args = [lengths, both_gains, own, far, *pieces, *before]
    half = own.shape[0]
    sums = [shape(half, 2 * PARTS * HD), shape(half, 2 * HD, F32)]
    if part == 0:
        out_shape = [shape(BLK, 2 * WIDTH)] * YS + [*sums, shape(2, HD, F32)]
    else:
        out_shape = [shape(BLK, 2 * PARTS * WIDTH)] * YS + sums
        out_shape += [jax.ShapeDtypeStruct((others, 2, HD), F32)]
    scratch = [
        pltpu.VMEM((span, HD), BF16),
        pltpu.VMEM((span, HD), BF16),
        pltpu.VMEM((PAIR, span, HD), F32),
        pltpu.VMEM((PAIR, span, HD), F32),
        pltpu.VMEM((GROUP * half, HD), F32),
        pltpu.VMEM((GROUP * half, HD), F32),
        pltpu.VMEM((GROUP * half, HD), BF16),
        pltpu.VMEM((GROUP * half, HD), BF16),
        pltpu.VMEM((GROUP * half, HD), F32),
    ]
    scratch += [pltpu.VMEM((GROUP * half, HD), BF16)]
    return pl.pallas_call(
        functools.partial(attend_kernel, part),
        out_shape=out_shape,
        in_specs=specs([pltpu.SMEM] + [VMEM] * (len(args) - 1)),
        out_specs=specs([VMEM] * len(out_shape)),
        scratch_shapes=scratch,
        compiler_params=LIMIT,
        cost_estimate=pl.CostEstimate(
            flops=10 * 2 * GROUP * half * 384 * HD, bytes_accessed=4 << 20, transcendentals=GROUP * half * 384
        ),
    )(*args)


def finish_kv_kernel(both_gains_ref, kv_ref, *refs):
    own, far_ref, gains_ref, refs = refs[:PARTS], refs[PARTS], refs[PARTS + 1], refs[PARTS + 2 :]
    outs = refs[:YS]
    y_ref = refs[YS]
    k_gain = both_gains_ref[1:2, :]
    for p in range(PARTS):
        k_at = slice(p * HD, (p + 1) * HD)
        v_at = slice((PARTS + p) * HD, (PARTS + p + 1) * HD)
        unit, inverse = unit_of(kv_ref[:, k_at])
        dk = own[p][:, :HD] + far_ref[:, k_at].astype(F32)
        y_ref[:, k_at] = norm_back(dk, unit, inverse, k_gain).astype(BF16)
        y_ref[:, v_at] = (own[p][:, HD:] + far_ref[:, v_at].astype(F32)).astype(BF16)
    rest = jnp.concatenate([jnp.sum(gains_ref[...], axis=0), jnp.zeros((TAIL - 2, HD), F32)], axis=0)
    for step in range(YS):
        outs[step][:BLK, :] = y_ref[block_rows(ahead(step)), :]
        outs[step][BLK:, 3 * HD :] = jnp.zeros((TAIL, HD), BF16)
    for n in range(3):
        term = rest.astype(BF16)
        rest = rest - term.astype(F32)
        for step in range(YS):
            outs[step][BLK:, n * HD : (n + 1) * HD] = term


def unpack_moves(half, pieces, results):
    moves = []
    for step in range(YS):
        for n, result in enumerate(results):
            at = pl.ds(pl.multiple_of(behind(step) * half, half), half)
            moves.append((pieces[step].at[pl.ds(0, BLK), pl.ds(n * half, half)], result.at[:, at]))
    return moves


def unpack_qg_kernel(*refs):
    do_copies(unpack_moves(PARTS * WIDTH, refs[:YS], refs[YS:-1]), refs[-1])


def unpack_kv_kernel(scales, *refs):
    pieces = refs[:YS]
    dk_ref, dv_ref, q_ref, k_ref, sums_ref, sems = refs[YS:]
    started = start_copies(unpack_moves(PARTS * HD, pieces, (dk_ref, dv_ref)), sems)
    for step in range(YS):
        tail = pieces[step][BLK:, :].astype(F32)
        whole = (tail[:, :HD] + tail[:, HD : 2 * HD]) + tail[:, 2 * HD : 3 * HD]
        sums_ref[pl.ds(behind(step), 1)] = whole[None]
    total = (sums_ref[0] + sums_ref[1]) + (sums_ref[2] + sums_ref[3])
    q_ref[...] = total[0:1] * scales[0]
    k_ref[...] = total[1:2] * scales[1]
    for move in started:
        move.wait()


def over_y(pieces):
    moved = [pieces[0]]
    for step in range(1, YS):
        moved.append(
            lax.ppermute(
                pieces[step],
                "head",
                [(2 * y + c, 2 * ((y + step) % YS) + c) for y in range(YS) for c in range(2)],
            )
        )
    return moved


def over_x(x):
    return lax.ppermute(x, "head", [(i, i ^ 1) for i in range(2 * YS)])


def on_device(query, key_states, value_states, grad_attended, query_gain, key_gain, doc_lengths):
    replicas = lax.axis_size("dp")
    members = lax.axis_size("head")
    rows = query.shape[0]
    half = YS * rows
    wide = 2 * PARTS * HD

    pieces = pl.pallas_call(
        pack_kv_kernel,
        out_shape=[shape(rows, wide)] * YS,
        in_specs=specs([HBM] * 2),
        out_specs=specs([VMEM] * YS),
        scratch_shapes=[pltpu.SemaphoreType.DMA((2 * YS,))],
        compiler_params=PACK_LIMIT,
    )(key_states, value_states)
    kv_moved = over_y(pieces)
    soon, *pieces = pl.pallas_call(
        pack_qg_kernel,
        out_shape=[jax.ShapeDtypeStruct((YS, rows, 2 * WIDTH), BF16)] + [shape(rows, 2 * WIDTH)] * YS,
        in_specs=specs([HBM] * 2 + [VMEM]),
        out_specs=specs([VMEM] * (1 + YS)),
        scratch_shapes=[pltpu.SemaphoreType.DMA((4 * YS,))],
        compiler_params=LIMIT,
    )(query, grad_attended, kv_moved[1])
    qg_moved = over_y(pieces)
    own, both_gains = pl.pallas_call(
        gather_kv_kernel,
        out_shape=[shape(half, wide), shape(2, HD, F32)],
        in_specs=specs([VMEM] * (2 + YS)),
        out_specs=specs([VMEM] * 2),
        compiler_params=LIMIT,
    )(query_gain.reshape(1, HD), key_gain.reshape(1, HD), *kv_moved)
    far = over_x(own)
    groups = [[2 * y + c for y in range(YS)] for c in range(2)]
    soon = after(soon, both_gains)
    soon = lax.all_to_all(soon, "head", split_axis=0, concat_axis=0, tiled=True, axis_index_groups=groups)
    qg_parts = [[soon.reshape(half, 2 * WIDTH)], qg_moved]

    before = ()
    own_sums = []
    for part in range(PARTS):
        *outs, far_sum, own_sum, gains = attend(
            part, doc_lengths, both_gains, own, far, qg_parts[part], before, 2 * replicas
        )
        before = (*outs, far_sum, gains)
        own_sums.append(own_sum)
    far_back = over_x(far_sum)
    outs = over_y(outs)
    same_y = [[d * members + 2 * y + c for d in range(replicas) for c in range(2)] for y in range(YS)]
    gains = lax.all_to_all(
        gains, ("dp", "head"), split_axis=0, concat_axis=0, tiled=True, axis_index_groups=same_y
    )
    kv_back = pl.pallas_call(
        finish_kv_kernel,
        out_shape=[shape(rows + TAIL, wide)] * YS,
        in_specs=specs([VMEM] * (4 + PARTS)),
        out_specs=specs([VMEM] * YS),
        scratch_shapes=[pltpu.VMEM((half, wide), BF16)],
        compiler_params=LIMIT,
    )(both_gains, own, *own_sums, far_back, gains)
    kv_back = over_y(kv_back)
    out, dq = pl.pallas_call(
        unpack_qg_kernel,
        out_shape=[shape(rows, H * HD)] * 2,
        in_specs=specs([VMEM] * YS),
        out_specs=specs([HBM] * 2),
        scratch_shapes=[pltpu.SemaphoreType.DMA((2 * YS,))],
        compiler_params=LIMIT,
    )(*outs)
    all_tokens = rows * replicas * members
    scales = ((all_tokens * H) ** (-0.5), (all_tokens * KVH) ** (-0.5))
    dk, dv, q_total, k_total = pl.pallas_call(
        functools.partial(unpack_kv_kernel, scales),
        out_shape=[shape(rows, KVH * HD)] * 2 + [shape(1, HD, F32)] * 2,
        in_specs=specs([VMEM] * YS),
        out_specs=specs([HBM] * 2 + [VMEM] * 2),
        scratch_shapes=[pltpu.VMEM((YS, TAIL, HD), F32), pltpu.SemaphoreType.DMA((2 * YS,))],
        compiler_params=LIMIT,
    )(*kv_back)
    return out, dq, dk, dv, q_total.reshape(HD), k_total.reshape(HD)


def solution(mesh):
    rows = P(("dp", "head"), None)
    in_specs = (rows, rows, rows, rows, P(), P(), P())
    out_specs = (rows, rows, rows, rows, P(), P())
    return jax.shard_map(
        on_device, mesh=mesh, in_specs=in_specs, out_specs=out_specs, check_vma=False
    )
```
